32 devices in a mesh: grp: 8 (over z, x), sub: 4 (over y, core).
Axes of the slice: x: 2, y: 2, z: 4, core: 2. Of those that a mesh axis runs over, the one named last changes fastest.
Arguments:
- ocean_state: bfloat16 [8, 131072], P(None, ('grp', 'sub')), may hold values from -6 to 6
- ocean_area: float32 [131072], P(('grp', 'sub')), may hold values from 0.3 to 3
- atm_flux: bfloat16 [12, 32768], P(None, ('grp', 'sub')), may hold values from -6 to 6
- atm_area: float32 [32768], P(('grp', 'sub')), may hold values from 0.3 to 3
- coupling: float32 [12, 8], replicated, may hold values from -2 to 2
- remap_weight: bfloat16 [256, 12, 128, 128], P(('grp', 'sub')), may hold values from -0.21875 to 0.21875
- send_block: int32 [32, 3, 4, 6], P(('grp', 'sub')), may hold values from 0 to 31
- send_count: int32 [32, 3, 4], P(('grp', 'sub')), may hold values from 2 to 6, as said below
- link_slot: int32 [256, 12], P(('grp', 'sub')), may hold values from 0 to 71, as said below
- link_count: int32 [256], P(('grp', 'sub')), may hold values from 1 to 12, as said below
Outputs:
- state_on_atm: bfloat16 [8, 32768], P(None, ('grp', 'sub'))
- flux_on_ocean: bfloat16 [12, 131072], P(None, ('grp', 'sub'))
- imbalance: float32 [12], replicated
The draws below stay inside these ranges and needn't reach their ends.
Inputs may be any that keep to these rules, and one draw needn't show every extreme that they name: `send_count`: every rank has one route with exactly 6 live slots. `link_slot`: the 12 slots of one atmosphere block differ, and each is a live slot of the sending route. `link_count`: every rank has an atmosphere block with all 12 links live.
All inputs are finite; a program needn't handle non-finite values.
Results may differ from the reference program's by a relative error of at most 0.0075.
Values may be sent and summed in bfloat16 or wider, within the bound.
A program may use at most 64 MiB of HBM per device.

```python
import math
import jax
import jax.numpy as jnp
from jax import lax

FO = 8
FA = 12
BLK = 128
LINKS = 12
CAP = 6
OB = 32
AB = 8
OCELLS = 131072
ACOLS = 32768
ABLOCKS = 256
N_GRP = 8
N_SUB = 4


def route_counts(key):
    devices = N_GRP * N_SUB
    count_key = jax.random.fold_in(key, 101)
    base_counts = jax.random.randint(count_key, (devices, 3 * N_SUB), 2, CAP + 1)
    full_route = jax.random.randint(jax.random.fold_in(count_key, 1), (devices, 1), 0, 3 * N_SUB)
    route_ids = jnp.arange(3 * N_SUB, dtype=jnp.int32)[None, :]
    filled = jnp.where(route_ids == full_route, CAP, base_counts)
    return filled.reshape(devices, 3, N_SUB).astype(jnp.int32)


def draw_send_count(key, part):
    return route_counts(key)


def draw_link_slot(key, part):
    counts = route_counts(key)
    key = jax.random.fold_in(key, 7)
    devices = N_GRP * N_SUB
    slot_total = 3 * N_SUB * CAP
    rank_ids = jnp.arange(devices, dtype=jnp.int32)
    grp_of = rank_ids // N_SUB
    sub_of = rank_ids % N_SUB
    offsets = jnp.arange(3, dtype=jnp.int32)
    sub_ids = jnp.arange(N_SUB, dtype=jnp.int32)
    sources = (grp_of[:, None, None] + offsets[None, :, None] - 1) % N_GRP * N_SUB + sub_ids[None, None, :]
    row_ids = 2 - offsets
    got = counts[sources, row_ids[None, :, None], sub_of[:, None, None]]
    alive_slot = jnp.arange(CAP, dtype=jnp.int32)[None, None, None, :] < got[..., None]
    alive_slot = alive_slot.reshape(devices, 1, slot_total)
    scores = jax.random.randint(key, (devices, AB, slot_total), 0, 1 << 20) * slot_total + jnp.arange(slot_total, dtype=jnp.int32)
    scores = jnp.where(alive_slot, scores, -1)
    chosen = jax.lax.top_k(scores, LINKS)[1]
    return chosen.reshape(devices * AB, LINKS).astype(jnp.int32)


def draw_link_count(key, part):
    key = jax.random.fold_in(key, 13)
    devices = N_GRP * N_SUB
    base_counts = jax.random.randint(key, (devices, AB), 1, LINKS + 1)
    full_block = jax.random.randint(jax.random.fold_in(key, 1), (devices, 1), 0, AB)
    block_ids = jnp.arange(AB, dtype=jnp.int32)[None, :]
    return jnp.where(block_ids == full_block, LINKS, base_counts).reshape(devices * AB).astype(jnp.int32)


def with_ends(entries, key, smallest, largest):
    dims = entries.shape
    index_at = [jax.random.randint(jax.random.fold_in(key, axis), (), 0, dims[axis]) for axis in range(len(dims))]
    entries = entries.at[tuple(index_at)].set(smallest)
    longest = dims.index(max(dims))
    index_at[longest] = (index_at[longest] + 1) % dims[longest]
    return entries.at[tuple(index_at)].set(largest)


def shard_levels(own_key, shape, pieces, low, top_value):
    factor_of = 1.0
    for position, shards_of in pieces:
        steps = jax.random.uniform(jax.random.fold_in(jax.random.fold_in(own_key, 6), position), (shards_of,), jnp.float32, low / len(pieces), top_value / len(pieces))
        factor_of = factor_of * jnp.repeat(jnp.exp(steps), shape[position] // shards_of).reshape((-1,) + (1,) * (len(shape) - 1 - position))
    return factor_of


def noise(stream_key, dims, deviation, most, shards=(), kind=jnp.bfloat16):
    array = jax.random.normal(stream_key, dims, jnp.float32) * deviation
    if len(shards) > 0:
        array = shard_levels(stream_key, dims, shards, -0.22, 0.18) * array
    return jnp.clip(array, min=-most, max=most).astype(kind)


def setup_inputs(seed: int = 0) -> dict:
    keys = jax.random.split(jax.random.key(seed), 11)
    ocean_state = noise(keys[0], (FO, OCELLS), 1.0, 6.0, ((1, 32),))
    ocean_area = jnp.clip(jnp.exp(math.log(3.0) - 2.3025851 * jax.random.uniform(keys[1], (OCELLS,), jnp.float32) ** shard_levels(keys[1], (OCELLS,), ((0, 32),), -0.2, 0.2)), 0.3, 3.0)
    atm_flux = noise(keys[2], (FA, ACOLS), 1.0, 6.0, ((1, 32),))
    atm_area = jnp.clip(jnp.exp(math.log(3.0) - 2.3025851 * jax.random.uniform(keys[3], (ACOLS,), jnp.float32) ** shard_levels(keys[3], (ACOLS,), ((0, 32),), -0.2, 0.2)), 0.3, 3.0)
    coupling = noise(keys[4], (FA, FO), FO ** -0.5, 2.0, (), jnp.float32)
    remap_weight = noise(keys[5], (ABLOCKS, LINKS, BLK, BLK), (BLK * LINKS // 2) ** -0.5, 0.21875, ((0, 32),))
    send_block = with_ends(jax.random.randint(keys[6], (N_GRP * N_SUB, 3, N_SUB, CAP), 0, OB), jax.random.fold_in(keys[6], 1), 0, OB - 1).astype(jnp.int32)
    send_count = draw_send_count(jax.random.fold_in(keys[10], 71), 0)
    link_slot = draw_link_slot(jax.random.fold_in(keys[10], 71), 0)
    link_count = draw_link_count(jax.random.fold_in(keys[10], 71), 0)
    return {"ocean_state": ocean_state, "ocean_area": ocean_area, "atm_flux": atm_flux, "atm_area": atm_area, "coupling": coupling, "remap_weight": remap_weight, "send_block": send_block, "send_count": send_count, "link_slot": link_slot, "link_count": link_count}


def reference(ocean_state, ocean_area, atm_flux, atm_area, coupling, remap_weight, send_block, send_count, link_slot, link_count):
    devices = N_GRP * N_SUB
    slot_total = 3 * N_SUB * CAP
    blocks = ocean_state.reshape(FO, devices, OB, BLK)
    cap_ids = jnp.arange(CAP, dtype=jnp.int32)
    live_send = cap_ids[None, None, None, :] < send_count[:, :, :, None]
    rank_ids = jnp.arange(devices, dtype=jnp.int32)
    grp_of = rank_ids // N_SUB
    sub_of = rank_ids % N_SUB
    offsets = jnp.arange(3, dtype=jnp.int32)
    sub_ids = jnp.arange(N_SUB, dtype=jnp.int32)
    peers = (grp_of[:, None, None] + offsets[None, :, None] - 1) % N_GRP * N_SUB + sub_ids[None, None, :]
    row_ids = (2 - offsets).astype(jnp.int32)
    weights = remap_weight.reshape(devices, AB, LINKS, BLK, BLK)
    slot_of = link_slot.reshape(devices, AB, LINKS)
    used_of = jnp.arange(LINKS, dtype=jnp.int32)[None, None, :] < link_count.reshape(devices, AB)[:, :, None]
    fluxes = atm_flux.reshape(FA, devices, AB, BLK).transpose(1, 0, 2, 3)
    atm_areas = atm_area.reshape(devices, AB, BLK)

    def receive(inputs):
        peer_here, sub_here, weight, slot_ids, used_link, flux_here, area_here = inputs
        picked = send_block[peer_here[:, :, None], row_ids[:, None, None], sub_here, cap_ids[None, None, :]]
        alive_slot = live_send[peer_here[:, :, None], row_ids[:, None, None], sub_here, cap_ids[None, None, :]]
        arrived = blocks[:, peer_here[:, :, None], picked]
        arrived = jnp.where(alive_slot[None, :, :, :, None], arrived, jnp.zeros((), arrived.dtype)).reshape(FO, slot_total, BLK)
        taken = arrived[:, slot_ids]
        taken = jnp.where(used_link[None, :, :, None], taken, jnp.zeros((), taken.dtype))
        weight_wide = weight.astype(jnp.float32)
        state_sum = jnp.einsum('falr,alrq->faq', taken.astype(jnp.float32), weight_wide, precision=lax.Precision.HIGHEST)
        coupled = (flux_here.astype(jnp.float32) + jnp.einsum('gf,faq->gaq', coupling, state_sum, precision=lax.Precision.HIGHEST)).astype(jnp.bfloat16)
        link_part = jnp.einsum('gaq,alrq->algr', coupled.astype(jnp.float32), weight_wide, precision=lax.Precision.HIGHEST)
        link_part = jnp.where(used_link[:, :, None, None], link_part, jnp.zeros((), link_part.dtype))
        slot_part = jax.ops.segment_sum(link_part.reshape(AB * LINKS, FA, BLK), slot_ids.reshape(-1), num_segments=slot_total).astype(jnp.bfloat16)
        atm_part = lax.optimization_barrier(jnp.sum(area_here[None] * coupled.astype(jnp.float32), axis=(1, 2)))
        return (state_sum.astype(jnp.bfloat16), slot_part, atm_part)
    states, slot_parts, atm_parts = lax.map(receive, (peers, sub_of, weights, slot_of, used_of, fluxes, atm_areas))
    slot_parts = slot_parts.reshape(devices, 3, N_SUB, CAP, FA, BLK)
    ocean_areas = ocean_area.reshape(devices, OB, BLK)
    block_ids = jnp.arange(OB, dtype=jnp.int32)

    def collect(inputs):
        peer_here, sub_here, picks, alive_slot, area_here = inputs
        returned = slot_parts[peer_here[:, :, None], row_ids[:, None, None], sub_here, cap_ids[None, None, :]]
        block_hits = ((picks[..., None] == block_ids) & alive_slot[..., None]).reshape(slot_total, OB)
        block_hits = jnp.where(block_hits, 1.0, 0.0).astype(jnp.float32)
        flux_sum = jnp.einsum('sb,sgr->gbr', block_hits, returned.reshape(slot_total, FA, BLK).astype(jnp.float32), precision=lax.Precision.HIGHEST)
        return (flux_sum, lax.optimization_barrier(jnp.sum(area_here[None] * flux_sum, axis=(1, 2))))
    flux_parts, ocean_parts = lax.map(collect, (peers, sub_of, send_block, live_send, ocean_areas))
    state_on_atm = states.transpose(1, 0, 2, 3).reshape(FO, devices * AB * BLK)
    flux_on_ocean = flux_parts.transpose(1, 0, 2, 3).reshape(FA, devices * OB * BLK).astype(jnp.bfloat16)
    norm_scale = 1.0 / math.sqrt(devices * AB * BLK)
    imbalance = (lax.optimization_barrier(jnp.sum(atm_parts, axis=0)) - lax.optimization_barrier(jnp.sum(ocean_parts, axis=0))) * norm_scale
    return (state_on_atm, flux_on_ocean, imbalance)
```

```python
import functools
import math

import jax
import jax.numpy as jnp
from jax import lax
from jax.experimental import pallas as pl
from jax.experimental.pallas import tpu as pltpu
from jax.sharding import PartitionSpec as P

MESH = pl.DeviceIdType.MESH


def kernel(
    groups,
    subs,
    norm_scale,
    state_hbm,
    ocean_area_hbm,
    flux_hbm,
    atm_area_hbm,
    coupling_hbm,
    weight_hbm,
    block_hbm,
    count_hbm,
    link_slot_hbm,
    link_count_hbm,
    state_out,
    flux_out,
    imbalance_out,
    state_in,
    ocean_area_in,
    flux_in,
    atm_area_in,
    coupling_in,
    weight_in,
    block_in,
    count_in,
    link_slot_in,
    link_count_in,
    state_wide,
    state_send,
    state_recv,
    arrived,
    area_send,
    area_recv,
    parts,
    slot_hits,
    chooser,
    flux_send,
    flux_recv,
    sub_parts,
    grp_parts,
    load_sem,
    state_sems,
    area_sems,
    flux_sems,
    sub_sems,
    grp_sems,
):
    f32, bf16, i32 = jnp.float32, jnp.bfloat16, jnp.int32
    ocean_blocks = state_wide.shape[0]
    fields_ocean = state_wide.shape[1]
    width = state_wide.shape[2]
    fields_atm = flux_in.shape[0]
    atm_blocks, link_total = weight_in.shape[:2]
    capacity = block_in.shape[3]
    routes = 3 * subs
    links = atm_blocks * link_total
    quad_rows = 4 * capacity
    flux_rows = flux_send.shape[1]
    me_grp = lax.axis_index("grp")
    me_sub = lax.axis_index("sub")

    pairs = [
        (block_hbm, block_in),
        (count_hbm, count_in),
        (state_hbm, state_in),
        (ocean_area_hbm, ocean_area_in),
        (link_slot_hbm, link_slot_in),
        (link_count_hbm, link_count_in),
        (coupling_hbm, coupling_in),
        (flux_hbm, flux_in),
        (atm_area_hbm, atm_area_in),
        (weight_hbm, weight_in),
    ]
    loads = [
        pltpu.make_async_copy(source, target, load_sem.at[n])
        for n, (source, target) in enumerate(pairs)
    ]
    for load in loads:
        load.start()

    steps = [(o, t) for o in (0, 2) for t in range(subs)] + [(1, t) for t in range(1, subs)]

    def grp_at(offset):
        return lax.rem(me_grp + offset + groups, groups)

    def sub_at(t):
        return lax.rem(me_sub + t, subs)

    barrier = pltpu.get_barrier_semaphore()
    partners = [(grp_at(o - 1), sub_at(t)) for o, t in steps]
    partners += [(grp_at(d), me_sub) for d in range(2, groups - 1)]
    for partner in partners:
        pl.semaphore_signal(barrier, inc=1, device_id=partner, device_id_type=MESH)

    def exchange(source, target, sems, o, t):
        k = sub_at(t)
        return pltpu.make_async_remote_copy(
            src_ref=source.at[o * subs + k],
            dst_ref=target.at[(2 - o) * subs + me_sub],
            send_sem=sems.at[0, o, t],
            recv_sem=sems.at[1, o, t],
            device_id=(grp_at(o - 1), k),
            device_id_type=MESH,
        )

    for n in range(3):
        loads[n].wait()
    for b in range(ocean_blocks):
        state_wide[b] = state_in[:, b * width : (b + 1) * width].astype(f32)

    def alive(o, k, c):
        return jnp.where(c < count_in[0, o, k], 1.0, 0.0).astype(f32)

    def fill_state(o, t):
        k = sub_at(t)
        rows = [
            state_wide[block_in[0, o, k, c]] * alive(o, k, c) for c in range(capacity)
        ]
        return jnp.concatenate(rows, axis=0).astype(bf16)

    state_copies = []
    for n, (o, t) in enumerate(steps):
        state_send[o * subs + sub_at(t)] = fill_state(o, t)
        if n == 0:
            pl.semaphore_wait(barrier, len(partners))
        copy = exchange(state_send, state_recv, state_sems, o, t)
        copy.start()
        state_copies.append(copy)
    state_recv[subs + me_sub] = fill_state(1, 0)

    loads[3].wait()
    area_copies = []
    for o, t in steps + [(1, 0)]:
        k = sub_at(t)
        target = area_recv if (o, t) == (1, 0) else area_send
        for c in range(capacity):
            target[o * subs + k, c : c + 1, :] = ocean_area_in[block_in[0, o, k, c]] * alive(
                o, k, c
            )
        if (o, t) != (1, 0):
            copy = exchange(area_send, area_recv, area_sems, o, t)
            copy.start()
            area_copies.append(copy)

    for n in range(4, 9):
        loads[n].wait()
    lane = lax.broadcasted_iota(i32, (1, 4 * links), 1)
    link_of = lane % links
    quad_of = lane // links
    key = jnp.full((1, 4 * links), -1, i32)
    for a in range(atm_blocks):
        for l in range(link_total):
            slot = link_slot_in[a, l]
            row = (slot // capacity) * quad_rows + slot % capacity
            row = jnp.where(l < link_count_in[a], row, -quad_rows)
            key = jnp.where(link_of == a * link_total + l, row, key)
    key = key + quad_of * capacity
    key = jnp.where(key < 0, -1, key)
    row_of = lax.broadcasted_iota(i32, (routes * quad_rows, 4 * links), 0)
    slot_hits[...] = jnp.where(row_of == key, 1.0, 0.0).astype(bf16)

    lane = lax.broadcasted_iota(i32, (1, routes * flux_rows), 1)
    inner = lane % flux_rows
    slot_of = (lane // flux_rows) * capacity + inner % capacity
    key = jnp.full((1, routes * flux_rows), -1, i32)
    for o in range(3):
        for k in range(subs):
            for c in range(capacity):
                block = jnp.where(c < count_in[0, o, k], block_in[0, o, k, c] * 16, -32)
                key = jnp.where(slot_of == (o * subs + k) * capacity + c, block, key)
    key = key + inner // capacity
    key = jnp.where(inner < fields_atm * capacity, key, -1)
    for part in range(4):
        rows = ocean_blocks * 4
        row_of = lax.broadcasted_iota(i32, (rows, routes * flux_rows), 0) + part * rows
        chooser[part * rows : (part + 1) * rows, :] = jnp.where(row_of == key, 1.0, 0.0).astype(
            bf16
        )
    coefficient = [
        jnp.broadcast_to(coupling_in[:, f : f + 1], (fields_atm, width))
        for f in range(fields_ocean)
    ]

    for copy in state_copies:
        copy.wait_recv()
    loads[9].wait()
    for p in range(routes):
        arrived[p * capacity : (p + 1) * capacity] = (
            state_recv[p].astype(f32).reshape(capacity, fields_ocean, width)
        )

    atm_acc = jnp.zeros((fields_atm, width), f32)
    for a in range(atm_blocks):
        taken = []
        for l in range(link_total):
            used = jnp.where(l < link_count_in[a], 1.0, 0.0).astype(f32)
            taken.append(arrived[link_slot_in[a, l]] * used)
        taken = jnp.concatenate(taken, axis=1).astype(bf16)
        weight = weight_in[a].reshape(link_total * width, width)
        state_sum = jnp.dot(taken, weight, preferred_element_type=f32)
        here = slice(a * width, (a + 1) * width)
        state_out[:, here] = state_sum.astype(bf16)
        value = flux_in[:, here].astype(f32)
        change = coefficient[0] * state_sum[0:1]
        for f in range(1, fields_ocean):
            change = change + coefficient[f] * state_sum[f : f + 1]
        coupled = (value + change).astype(bf16)
        atm_acc = atm_acc + atm_area_in[a : a + 1, :] * coupled.astype(f32)
        part = lax.dot_general(
            coupled, weight, (((1,), (1,)), ((), ())), preferred_element_type=f32
        )
        for l in range(link_total):
            parts[pl.ds(a * link_total + l, fields_atm, stride=links), :] = part[
                :, l * width : (l + 1) * width
            ]

    quads = []
    for q in range(fields_atm // 4):
        operand = parts[q * 4 * links : (q + 1) * 4 * links, :].astype(bf16)
        quads.append(jnp.dot(slot_hits[...], operand, preferred_element_type=f32))
    blank = jnp.zeros((flux_rows - fields_atm * capacity, width), f32)
    for p in range(routes):
        rows = [quad[p * quad_rows : (p + 1) * quad_rows] for quad in quads]
        flux_send[p] = jnp.concatenate(rows + [blank], axis=0).astype(bf16)
    flux_copies = []
    for o, t in steps:
        copy = exchange(flux_send, flux_recv, flux_sems, o, t)
        copy.start()
        flux_copies.append(copy)
    flux_recv[subs + me_sub] = flux_send[subs + me_sub]

    for copy in area_copies:
        copy.wait_recv()
    ocean_acc = [jnp.zeros((quad_rows, width), f32) for _ in quads]
    for p in range(routes):
        area = area_recv[p][:capacity]
        area = jnp.concatenate([area] * 4, axis=0)
        for q, quad in enumerate(quads):
            rounded = quad[p * quad_rows : (p + 1) * quad_rows].astype(bf16).astype(f32)
            ocean_acc[q] = ocean_acc[q] + rounded * area

    def to_lanes(column, group):
        rows = column.shape[0]
        row_of = lax.broadcasted_iota(i32, (rows, 128), 0) // group
        lane_of = lax.broadcasted_iota(i32, (rows, 128), 1)
        return jnp.sum(jnp.where(row_of == lane_of, column, 0.0), axis=0, keepdims=True)

    ocean_rows = jnp.concatenate(ocean_acc, axis=0)
    mine = to_lanes(jnp.sum(atm_acc, axis=1, keepdims=True), 1) - to_lanes(
        jnp.sum(ocean_rows, axis=1, keepdims=True), capacity
    )
    sub_parts[me_sub] = jnp.broadcast_to(mine, (8, 128))
    sub_copies = []
    for t in range(1, subs):
        copy = pltpu.make_async_remote_copy(
            src_ref=sub_parts.at[me_sub],
            dst_ref=sub_parts.at[me_sub],
            send_sem=sub_sems.at[0, t],
            recv_sem=sub_sems.at[1, t],
            device_id=(me_grp, sub_at(t)),
            device_id_type=MESH,
        )
        copy.start()
        sub_copies.append(copy)
    for copy in sub_copies:
        copy.wait_recv()
    total = sub_parts[0]
    for k in range(1, subs):
        total = total + sub_parts[k]
    grp_parts[me_grp] = total
    grp_copies = []
    for d in range(1, groups):
        copy = pltpu.make_async_remote_copy(
            src_ref=grp_parts.at[me_grp],
            dst_ref=grp_parts.at[me_grp],
            send_sem=grp_sems.at[0, d],
            recv_sem=grp_sems.at[1, d],
            device_id=(grp_at(d), me_sub),
            device_id_type=MESH,
        )
        copy.start()
        grp_copies.append(copy)

    for copy in flux_copies:
        copy.wait_recv()
    returned = flux_recv[...].reshape(routes * flux_rows, width)
    flux_sum = jnp.dot(chooser[...], returned, preferred_element_type=f32)
    for b in range(ocean_blocks):
        flux_out[:, b * width : (b + 1) * width] = flux_sum[
            b * 16 : b * 16 + fields_atm
        ].astype(bf16)

    for copy in grp_copies:
        copy.wait_recv()
    total = grp_parts[0]
    for i in range(1, groups):
        total = total + grp_parts[i]
    imbalance_out[...] = total * norm_scale
    for copy in state_copies + area_copies + flux_copies + sub_copies + grp_copies:
        copy.wait_send()


def shards(
    groups,
    subs,
    ocean_state,
    ocean_area,
    atm_flux,
    atm_area,
    coupling,
    remap_weight,
    send_block,
    send_count,
    link_slot,
    link_count,
):
    f32, bf16, i32 = jnp.float32, jnp.bfloat16, jnp.int32
    fields_ocean = ocean_state.shape[0]
    fields_atm = atm_flux.shape[0]
    atm_blocks, link_total, width = remap_weight.shape[:3]
    ocean_blocks = ocean_state.shape[1] // width
    capacity = send_block.shape[3]
    routes = 3 * subs
    links = atm_blocks * link_total
    flux_rows = -(-fields_atm * capacity // 16) * 16
    norm_scale = 1.0 / math.sqrt(groups * subs * atm_blocks * width)
    anywhere = pl.BlockSpec(memory_space=pl.ANY)
    vmem = pl.BlockSpec(memory_space=pltpu.VMEM)
    state_on_atm, flux_on_ocean, imbalance = pl.pallas_call(
        functools.partial(kernel, groups, subs, norm_scale),
        out_shape=(
            jax.ShapeDtypeStruct((fields_ocean, atm_blocks * width), bf16),
            jax.ShapeDtypeStruct((fields_atm, ocean_blocks * width), bf16),
            jax.ShapeDtypeStruct((8, 128), f32),
        ),
        in_specs=[anywhere] * 10,
        out_specs=(vmem, vmem, vmem),
        scratch_shapes=[
            pltpu.VMEM(ocean_state.shape, bf16),
            pltpu.VMEM((ocean_blocks, 1, width), f32),
            pltpu.VMEM(atm_flux.shape, bf16),
            pltpu.VMEM((atm_blocks, width), f32),
            pltpu.VMEM(coupling.shape, f32),
            pltpu.VMEM(remap_weight.shape, bf16),
            pltpu.SMEM(send_block.shape, i32),
            pltpu.SMEM(send_count.shape, i32),
            pltpu.SMEM(link_slot.shape, i32),
            pltpu.SMEM(link_count.shape, i32),
            pltpu.VMEM((ocean_blocks, fields_ocean, width), f32),
            pltpu.VMEM((routes, capacity * fields_ocean, width), bf16),
            pltpu.VMEM((routes, capacity * fields_ocean, width), bf16),
            pltpu.VMEM((routes * capacity, fields_ocean, width), f32),
            pltpu.VMEM((routes, 8, width), f32),
            pltpu.VMEM((routes, 8, width), f32),
            pltpu.VMEM((fields_atm * links, width), f32),
            pltpu.VMEM((routes * 4 * capacity, 4 * links), bf16),
            pltpu.VMEM((ocean_blocks * 16, routes * flux_rows), bf16),
            pltpu.VMEM((routes, flux_rows, width), bf16),
            pltpu.VMEM((routes, flux_rows, width), bf16),
            pltpu.VMEM((subs, 8, 128), f32),
            pltpu.VMEM((groups, 8, 128), f32),
            pltpu.SemaphoreType.DMA((10,)),
            pltpu.SemaphoreType.DMA((2, 3, subs)),
            pltpu.SemaphoreType.DMA((2, 3, subs)),
            pltpu.SemaphoreType.DMA((2, 3, subs)),
            pltpu.SemaphoreType.DMA((2, subs)),
            pltpu.SemaphoreType.DMA((2, groups)),
        ],
        compiler_params=pltpu.CompilerParams(
            collective_id=0, has_side_effects=True, vmem_limit_bytes=40 * 1024 * 1024
        ),
    )(
        ocean_state,
        ocean_area.reshape(ocean_blocks, 1, width),
        atm_flux,
        atm_area.reshape(atm_blocks, width),
        coupling,
        remap_weight,
        send_block,
        send_count,
        link_slot,
        link_count,
    )
    return state_on_atm, flux_on_ocean, imbalance[0, :fields_atm]


def solution(mesh):
    placed = (
        P(None, ("grp", "sub")),
        P(("grp", "sub")),
        P(None, ("grp", "sub")),
        P(("grp", "sub")),
        P(),
        P(("grp", "sub"), None, None, None),
        P(("grp", "sub"), None, None, None),
        P(("grp", "sub"), None, None),
        P(("grp", "sub"), None),
        P(("grp", "sub")),
    )
    return jax.shard_map(
        functools.partial(shards, mesh.shape["grp"], mesh.shape["sub"]),
        mesh=mesh,
        in_specs=placed,
        out_specs=(P(None, ("grp", "sub")), P(None, ("grp", "sub")), P()),
        check_vma=False,
    )
```

```python
import functools
import math

import jax
import jax.numpy as jnp
from jax import lax
from jax.experimental import pallas as pl
from jax.experimental.pallas import tpu as pltpu
from jax.sharding import PartitionSpec as P

MESH = pl.DeviceIdType.MESH
VMEM_BYTES = 60 * 1024 * 1024


def kernel(
    groups,
    subs,
    norm_scale,
    state_hbm,
    ocean_area_hbm,
    flux_hbm,
    atm_area_hbm,
    coupling_hbm,
    weight_hbm,
    block_hbm,
    count_hbm,
    link_slot_hbm,
    link_count_hbm,
    state_out_hbm,
    flux_out_hbm,
    imbalance_out,
    state_out,
    flux_out,
    state_in,
    ocean_area_in,
    flux_in,
    atm_area_in,
    coupling_in,
    weight_in,
    block_in,
    count_in,
    link_slot_in,
    link_count_in,
    picked,
    read_slot,
    state_wide,
    state_send,
    state_recv,
    arrived,
    area_send,
    area_recv,
    parts,
    slot_hits,
    chooser,
    flux_send,
    flux_recv,
    sub_parts,
    grp_parts,
    load_sem,
    state_sems,
    area_sems,
    flux_sems,
    sub_sems,
    grp_sems,
):
    f32, bf16, i32 = jnp.float32, jnp.bfloat16, jnp.int32
    ocean_blocks = ocean_area_hbm.shape[0]
    fields_ocean = state_wide.shape[1]
    width = state_wide.shape[2]
    fields_atm = flux_in.shape[0]
    atm_blocks, link_total = weight_in.shape[:2]
    capacity = block_in.shape[3]
    routes = 3 * subs
    links = atm_blocks * link_total
    quad_rows = 4 * capacity
    flux_rows = flux_send.shape[1]
    me_grp = lax.axis_index("grp")
    me_sub = lax.axis_index("sub")

    pairs = [
        (block_hbm, block_in),
        (count_hbm, count_in),
        (state_hbm, state_in),
        (ocean_area_hbm, ocean_area_in.at[pl.ds(0, ocean_area_hbm.shape[0])]),
        (link_slot_hbm, link_slot_in),
        (link_count_hbm, link_count_in),
        (coupling_hbm, coupling_in),
        (flux_hbm, flux_in),
        (atm_area_hbm, atm_area_in),
        (weight_hbm, weight_in),
    ]
    loads = [
        pltpu.make_async_copy(source, target, load_sem.at[n])
        for n, (source, target) in enumerate(pairs)
    ]
    for load in loads:
        load.start()

    steps = [(o, t) for o in (0, 2) for t in range(subs)] + [(1, t) for t in range(1, subs)]

    def grp_at(offset):
        return lax.rem(me_grp + offset + groups, groups)

    def sub_at(t):
        return lax.rem(me_sub + t, subs)

    barrier = pltpu.get_barrier_semaphore()
    partners = [(grp_at(o - 1), sub_at(t)) for o, t in steps]
    partners += [(grp_at(d), me_sub) for d in range(2, groups - 1)]
    for partner in partners:
        pl.semaphore_signal(barrier, inc=1, device_id=partner, device_id_type=MESH)

    def exchange(source, target, sems, o, t):
        k = sub_at(t)
        return pltpu.make_async_remote_copy(
            src_ref=source.at[o * subs + k],
            dst_ref=target.at[(2 - o) * subs + me_sub],
            send_sem=sems.at[0, o, t],
            recv_sem=sems.at[1, o, t],
            device_id=(grp_at(o - 1), k),
            device_id_type=MESH,
        )

    for n in range(3):
        loads[n].wait()
    for b in range(ocean_blocks):
        state_wide[b] = state_in[:, b * width : (b + 1) * width].astype(f32)
    state_wide[ocean_blocks] = jnp.zeros((fields_ocean, width), f32)

    def block_at(o, k, c):
        return jnp.where(c < count_in[o, 0, k], block_in[0, o, k, c], ocean_blocks)

    for o in range(3):
        for k in range(subs):
            for c in range(capacity):
                picked[(o * subs + k) * capacity + c] = block_at(o, k, c)

    state_copies = []
    for o in (0, 2, 1):
        for k in range(subs):
            first = (o * subs + k) * capacity
            rows = [state_wide[picked[first + c]] for c in range(capacity)]
            state_send[o * subs + k] = jnp.concatenate(rows, axis=0).astype(bf16)
        if o == 0:
            pl.semaphore_wait(barrier, len(partners))
        for t in range(1 if o == 1 else 0, subs):
            copy = exchange(state_send, state_recv, state_sems, o, t)
            copy.start()
            state_copies.append(copy)
    state_recv[subs + me_sub] = state_send[subs + me_sub]

    loads[3].wait()
    ocean_area_in[ocean_blocks] = jnp.zeros((1, width), f32)
    area_copies = []
    for o in (0, 2, 1):
        for k in range(subs):
            p = o * subs + k
            for c in range(capacity):
                area_send[p, c : c + 1, :] = ocean_area_in[picked[p * capacity + c]]
        for t in range(1 if o == 1 else 0, subs):
            copy = exchange(area_send, area_recv, area_sems, o, t)
            copy.start()
            area_copies.append(copy)
    area_recv[subs + me_sub] = area_send[subs + me_sub]

    for n in range(4, 9):
        loads[n].wait()
    lane = lax.broadcasted_iota(i32, (1, 4 * links), 1)
    link_of = lane % links
    quad_of = lane // links
    key = jnp.full((1, 4 * links), -1, i32)
    for a in range(atm_blocks):
        for l in range(link_total):
            slot = link_slot_in[a, l]
            used = l < link_count_in[a]
            read_slot[a * link_total + l] = jnp.where(used, slot, routes * capacity)
            row = (slot // capacity) * quad_rows + slot % capacity
            row = jnp.where(used, row, -quad_rows)
            key = jnp.where(link_of == a * link_total + l, row, key)
    key = key + quad_of * capacity
    key = jnp.where(key < 0, -1, key)
    row_of = lax.broadcasted_iota(i32, (routes * quad_rows, 4 * links), 0)
    slot_hits[...] = jnp.where(row_of == key, 1.0, 0.0).astype(bf16)

    lane = lax.broadcasted_iota(i32, (1, routes * flux_rows), 1)
    inner = lane % flux_rows
    slot_of = (lane // flux_rows) * capacity + inner % capacity
    key = jnp.full((1, routes * flux_rows), -1, i32)
    for o in range(3):
        for k in range(subs):
            for c in range(capacity):
                block = jnp.where(c < count_in[o, 0, k], block_in[0, o, k, c] * 16, -32)
                key = jnp.where(slot_of == (o * subs + k) * capacity + c, block, key)
    key = key + inner // capacity
    key = jnp.where(inner < fields_atm * capacity, key, -1)
    for part in range(4):
        rows = ocean_blocks * 4
        row_of = lax.broadcasted_iota(i32, (rows, routes * flux_rows), 0) + part * rows
        chooser[part * rows : (part + 1) * rows, :] = jnp.where(row_of == key, 1.0, 0.0).astype(
            bf16
        )
    row_of = lax.broadcasted_iota(i32, (fields_atm, fields_atm), 0)
    lane_of = lax.broadcasted_iota(i32, (fields_atm, fields_atm), 1)
    arrived[routes * capacity] = jnp.zeros((fields_ocean, width), f32)
    coefficient = []
    for f in range(fields_ocean):
        spread = jnp.where(row_of == lane_of, coupling_in[f : f + 1, :], 0.0)
        column = jnp.sum(spread, axis=1, keepdims=True)
        coefficient.append(jnp.broadcast_to(column, (fields_atm, width)))

    for copy in state_copies:
        copy.wait_recv()
    loads[9].wait()
    for p in range(routes):
        arrived[p * capacity : (p + 1) * capacity] = (
            state_recv[p].astype(f32).reshape(capacity, fields_ocean, width)
        )

    atm_acc = jnp.zeros((fields_atm, width), f32)
    for a in range(atm_blocks):
        taken = [arrived[read_slot[a * link_total + l]] for l in range(link_total)]
        taken = jnp.concatenate(taken, axis=1).astype(bf16)
        weight = weight_in[a].reshape(link_total * width, width)
        state_sum = jnp.dot(taken, weight, preferred_element_type=f32)
        here = slice(a * width, (a + 1) * width)
        state_out[:, here] = state_sum.astype(bf16)
        value = flux_in[:, here].astype(f32)
        change = coefficient[0] * state_sum[0:1]
        for f in range(1, fields_ocean):
            change = change + coefficient[f] * state_sum[f : f + 1]
        coupled = (value + change).astype(bf16)
        atm_acc = atm_acc + atm_area_in[a : a + 1, :] * coupled.astype(f32)
        part = lax.dot_general(
            coupled, weight, (((1,), (1,)), ((), ())), preferred_element_type=f32
        )
        for l in range(link_total):
            parts[pl.ds(a * link_total + l, fields_atm, stride=links), :] = part[
                :, l * width : (l + 1) * width
            ]

    state_store = pltpu.make_async_copy(state_out, state_out_hbm, load_sem.at[10])
    state_store.start()

    quads = []
    for q in range(fields_atm // 4):
        operand = parts[q * 4 * links : (q + 1) * 4 * links, :].astype(bf16)
        quads.append(jnp.dot(slot_hits[...], operand, preferred_element_type=f32))
    blank = jnp.zeros((flux_rows - fields_atm * capacity, width), f32)
    for p in range(routes):
        rows = [quad[p * quad_rows : (p + 1) * quad_rows] for quad in quads]
        flux_send[p] = jnp.concatenate(rows + [blank], axis=0).astype(bf16)
    flux_copies = []
    for o, t in steps:
        copy = exchange(flux_send, flux_recv, flux_sems, o, t)
        copy.start()
        flux_copies.append(copy)
    flux_recv[subs + me_sub] = flux_send[subs + me_sub]

    for copy in area_copies:
        copy.wait_recv()
    ocean_acc = [jnp.zeros((quad_rows, width), f32) for _ in quads]
    for p in range(routes):
        area = area_recv[p][:capacity]
        area = jnp.concatenate([area] * 4, axis=0)
        for q, quad in enumerate(quads):
            rounded = quad[p * quad_rows : (p + 1) * quad_rows].astype(bf16).astype(f32)
            ocean_acc[q] = ocean_acc[q] + rounded * area

    def to_lanes(column, group):
        rows = column.shape[0]
        row_of = lax.broadcasted_iota(i32, (rows, 128), 0) // group
        lane_of = lax.broadcasted_iota(i32, (rows, 128), 1)
        return jnp.sum(jnp.where(row_of == lane_of, column, 0.0), axis=0, keepdims=True)

    ocean_rows = jnp.concatenate(ocean_acc, axis=0)
    mine = to_lanes(jnp.sum(atm_acc, axis=1, keepdims=True), 1) - to_lanes(
        jnp.sum(ocean_rows, axis=1, keepdims=True), capacity
    )
    sub_parts[me_sub] = mine
    sub_copies = []
    for t in range(1, subs):
        copy = pltpu.make_async_remote_copy(
            src_ref=sub_parts.at[me_sub],
            dst_ref=sub_parts.at[me_sub],
            send_sem=sub_sems.at[0, t],
            recv_sem=sub_sems.at[1, t],
            device_id=(me_grp, sub_at(t)),
            device_id_type=MESH,
        )
        copy.start()
        sub_copies.append(copy)
    for copy in sub_copies:
        copy.wait_recv()
    total = sub_parts[0]
    for k in range(1, subs):
        total = total + sub_parts[k]
    grp_parts[me_grp] = total
    grp_copies = []
    for d in range(1, groups):
        copy = pltpu.make_async_remote_copy(
            src_ref=grp_parts.at[me_grp],
            dst_ref=grp_parts.at[me_grp],
            send_sem=grp_sems.at[0, d],
            recv_sem=grp_sems.at[1, d],
            device_id=(grp_at(d), me_sub),
            device_id_type=MESH,
        )
        copy.start()
        grp_copies.append(copy)

    for copy in flux_copies:
        copy.wait_recv()
    returned = flux_recv[...].reshape(routes * flux_rows, width)
    flux_sum = jnp.dot(chooser[...], returned, preferred_element_type=f32)
    for b in range(ocean_blocks):
        flux_out[:, b * width : (b + 1) * width] = flux_sum[
            b * 16 : b * 16 + fields_atm
        ].astype(bf16)

    flux_store = pltpu.make_async_copy(flux_out, flux_out_hbm, load_sem.at[11])
    flux_store.start()

    for copy in grp_copies:
        copy.wait_recv()
    total = grp_parts[0]
    for i in range(1, groups):
        total = total + grp_parts[i]
    imbalance_out[...] = total * norm_scale
    for copy in state_copies + area_copies + flux_copies + sub_copies + grp_copies:
        copy.wait_send()
    state_store.wait()
    flux_store.wait()


def finish(state_in, flux_in, total_in, state_out, flux_out, total_out, sems):
    copies = [
        pltpu.make_async_copy(flux_in, flux_out, sems.at[0]),
        pltpu.make_async_copy(state_in, state_out, sems.at[1]),
    ]
    for copy in copies:
        copy.start()
    total_out[...] = total_in[0, : total_out.shape[0]]
    for copy in copies:
        copy.wait()


def shards(
    groups,
    subs,
    ocean_state,
    ocean_area,
    atm_flux,
    atm_area,
    coupling,
    remap_weight,
    send_block,
    send_count,
    link_slot,
    link_count,
):
    f32, bf16, i32 = jnp.float32, jnp.bfloat16, jnp.int32
    fields_ocean = ocean_state.shape[0]
    fields_atm = atm_flux.shape[0]
    atm_blocks, link_total, width = remap_weight.shape[:3]
    ocean_blocks = ocean_state.shape[1] // width
    capacity = send_block.shape[3]
    routes = 3 * subs
    links = atm_blocks * link_total
    flux_rows = -(-fields_atm * capacity // 16) * 16
    norm_scale = 1.0 / math.sqrt(groups * subs * atm_blocks * width)
    anywhere = pl.BlockSpec(memory_space=pl.ANY)
    vmem = pl.BlockSpec(memory_space=pltpu.VMEM)
    state_on_atm, flux_on_ocean, imbalance = pl.pallas_call(
        functools.partial(kernel, groups, subs, norm_scale),
        out_shape=(
            jax.ShapeDtypeStruct((fields_ocean, atm_blocks * width), bf16),
            jax.ShapeDtypeStruct((fields_atm, ocean_blocks * width), bf16),
            jax.ShapeDtypeStruct((1, 128), f32),
        ),
        in_specs=[anywhere] * 10,
        out_specs=(anywhere, anywhere, vmem),
        scratch_shapes=[
            pltpu.VMEM((fields_ocean, atm_blocks * width), bf16),
            pltpu.VMEM((fields_atm, ocean_blocks * width), bf16),
            pltpu.VMEM(ocean_state.shape, bf16),
            pltpu.VMEM((ocean_blocks + 1, 1, width), f32),
            pltpu.VMEM(atm_flux.shape, bf16),
            pltpu.VMEM((atm_blocks, width), f32),
            pltpu.VMEM((fields_ocean, fields_atm), f32),
            pltpu.VMEM(remap_weight.shape, bf16),
            pltpu.SMEM(send_block.shape, i32),
            pltpu.SMEM((3, 1, subs), i32),
            pltpu.SMEM(link_slot.shape, i32),
            pltpu.SMEM(link_count.shape, i32),
            pltpu.SMEM((routes * capacity,), i32),
            pltpu.SMEM((links,), i32),
            pltpu.VMEM((ocean_blocks + 1, fields_ocean, width), f32),
            pltpu.VMEM((routes, capacity * fields_ocean, width), bf16),
            pltpu.VMEM((routes, capacity * fields_ocean, width), bf16),
            pltpu.VMEM((routes * capacity + 1, fields_ocean, width), f32),
            pltpu.VMEM((routes, 8, width), f32),
            pltpu.VMEM((routes, 8, width), f32),
            pltpu.VMEM((fields_atm * links, width), f32),
            pltpu.VMEM((routes * 4 * capacity, 4 * links), bf16),
            pltpu.VMEM((ocean_blocks * 16, routes * flux_rows), bf16),
            pltpu.VMEM((routes, flux_rows, width), bf16),
            pltpu.VMEM((routes, flux_rows, width), bf16),
            pltpu.VMEM((subs, 1, 128), f32),
            pltpu.VMEM((groups, 1, 128), f32),
            pltpu.SemaphoreType.DMA((12,)),
            pltpu.SemaphoreType.DMA((2, 3, subs)),
            pltpu.SemaphoreType.DMA((2, 3, subs)),
            pltpu.SemaphoreType.DMA((2, 3, subs)),
            pltpu.SemaphoreType.DMA((2, subs)),
            pltpu.SemaphoreType.DMA((2, groups)),
        ],
        compiler_params=pltpu.CompilerParams(
            collective_id=0, has_side_effects=True, vmem_limit_bytes=VMEM_BYTES
        ),
    )(
        ocean_state,
        ocean_area.reshape(ocean_blocks, 1, width),
        atm_flux,
        atm_area.reshape(atm_blocks, width),
        coupling.T,
        remap_weight,
        send_block,
        send_count.reshape(3, 1, subs),
        link_slot,
        link_count,
    )
    return pl.pallas_call(
        finish,
        out_shape=(
            jax.ShapeDtypeStruct(state_on_atm.shape, bf16),
            jax.ShapeDtypeStruct(flux_on_ocean.shape, bf16),
            jax.ShapeDtypeStruct((fields_atm,), f32),
        ),
        in_specs=[anywhere, anywhere, vmem],
        out_specs=(anywhere, anywhere, vmem),
        scratch_shapes=[pltpu.SemaphoreType.DMA((2,))],
        compiler_params=pltpu.CompilerParams(vmem_limit_bytes=VMEM_BYTES),
    )(state_on_atm, flux_on_ocean, imbalance)


def solution(mesh):
    placed = (
        P(None, ("grp", "sub")),
        P(("grp", "sub")),
        P(None, ("grp", "sub")),
        P(("grp", "sub")),
        P(),
        P(("grp", "sub"), None, None, None),
        P(("grp", "sub"), None, None, None),
        P(("grp", "sub"), None, None),
        P(("grp", "sub"), None),
        P(("grp", "sub")),
    )
    return jax.shard_map(
        functools.partial(shards, mesh.shape["grp"], mesh.shape["sub"]),
        mesh=mesh,
        in_specs=placed,
        out_specs=(P(None, ("grp", "sub")), P(None, ("grp", "sub")), P()),
        check_vma=False,
    )
```

```python
import functools
import math

import jax
import jax.numpy as jnp
from jax import lax
from jax.experimental import pallas as pl
from jax.experimental.pallas import tpu as pltpu
from jax.sharding import PartitionSpec as P

MESH = pl.DeviceIdType.MESH
VMEM_BYTES = 60 * 1024 * 1024


def kernel(
    groups,
    subs,
    norm_scale,
    state_hbm,
    ocean_area_hbm,
    flux_hbm,
    atm_area_hbm,
    coupling_hbm,
    weight_hbm,
    block_hbm,
    count_hbm,
    link_slot_hbm,
    link_count_hbm,
    state_out,
    flux_out,
    imbalance_out,
    state_in,
    ocean_area_in,
    flux_in,
    atm_area_in,
    coupling_in,
    weight_in,
    block_in,
    count_in,
    link_slot_in,
    link_count_in,
    picked,
    read_slot,
    state_wide,
    state_send,
    state_recv,
    arrived,
    area_send,
    area_recv,
    parts,
    slot_hits,
    chooser,
    flux_send,
    flux_recv,
    sub_parts,
    grp_parts,
    load_sem,
    state_sems,
    area_sems,
    flux_sems,
    sub_sems,
    grp_sems,
):
    f32, bf16, i32 = jnp.float32, jnp.bfloat16, jnp.int32
    ocean_blocks = ocean_area_hbm.shape[0]
    fields_ocean = state_wide.shape[1]
    width = state_wide.shape[2]
    fields_atm = flux_in.shape[0]
    atm_blocks, link_total = weight_in.shape[:2]
    capacity = block_in.shape[3]
    routes = 3 * subs
    links = atm_blocks * link_total
    quad_rows = 4 * capacity
    flux_rows = flux_send.shape[1]
    me_grp = lax.axis_index("grp")
    me_sub = lax.axis_index("sub")

    pairs = [
        (block_hbm, block_in),
        (count_hbm, count_in),
        (state_hbm, state_in),
        (ocean_area_hbm, ocean_area_in.at[pl.ds(0, ocean_area_hbm.shape[0])]),
        (link_slot_hbm, link_slot_in),
        (link_count_hbm, link_count_in),
        (coupling_hbm, coupling_in),
        (flux_hbm, flux_in),
        (atm_area_hbm, atm_area_in),
        (weight_hbm, weight_in),
    ]
    loads = [
        pltpu.make_async_copy(source, target, load_sem.at[n])
        for n, (source, target) in enumerate(pairs)
    ]
    for load in loads:
        load.start()

    steps = [(o, t) for o in (0, 2) for t in range(subs)] + [(1, t) for t in range(1, subs)]

    def grp_at(offset):
        return lax.rem(me_grp + offset + groups, groups)

    def sub_at(t):
        return lax.rem(me_sub + t, subs)

    barrier = pltpu.get_barrier_semaphore()
    partners = [(grp_at(o - 1), sub_at(t)) for o, t in steps]
    partners += [(grp_at(d), me_sub) for d in range(2, groups - 1)]
    for partner in partners:
        pl.semaphore_signal(barrier, inc=1, device_id=partner, device_id_type=MESH)

    def exchange(source, target, sems, o, t):
        k = sub_at(t)
        return pltpu.make_async_remote_copy(
            src_ref=source.at[o * subs + k],
            dst_ref=target.at[(2 - o) * subs + me_sub],
            send_sem=sems.at[0, o, t],
            recv_sem=sems.at[1, o, t],
            device_id=(grp_at(o - 1), k),
            device_id_type=MESH,
        )

    for n in range(3):
        loads[n].wait()
    for b in range(ocean_blocks):
        state_wide[b] = state_in[:, b * width : (b + 1) * width].astype(f32)
    state_wide[ocean_blocks] = jnp.zeros((fields_ocean, width), f32)

    def block_at(o, k, c):
        return jnp.where(c < count_in[o, 0, k], block_in[0, o, k, c], ocean_blocks)

    for o in range(3):
        for k in range(subs):
            for c in range(capacity):
                picked[(o * subs + k) * capacity + c] = block_at(o, k, c)

    state_copies = []
    for o in (0, 2, 1):
        for k in range(subs):
            first = (o * subs + k) * capacity
            rows = [state_wide[picked[first + c]] for c in range(capacity)]
            state_send[o * subs + k] = jnp.concatenate(rows, axis=0).astype(bf16)
        if o == 0:
            pl.semaphore_wait(barrier, len(partners))
        for t in range(1 if o == 1 else 0, subs):
            copy = exchange(state_send, state_recv, state_sems, o, t)
            copy.start()
            state_copies.append(copy)
    state_recv[subs + me_sub] = state_send[subs + me_sub]

    loads[3].wait()
    ocean_area_in[ocean_blocks] = jnp.zeros((1, width), f32)
    area_copies = []
    for o in (0, 2, 1):
        for k in range(subs):
            p = o * subs + k
            for c in range(capacity):
                area_send[p, c : c + 1, :] = ocean_area_in[picked[p * capacity + c]]
        for t in range(1 if o == 1 else 0, subs):
            copy = exchange(area_send, area_recv, area_sems, o, t)
            copy.start()
            area_copies.append(copy)
    area_recv[subs + me_sub] = area_send[subs + me_sub]

    for n in range(4, 9):
        loads[n].wait()
    lane = lax.broadcasted_iota(i32, (1, 4 * links), 1)
    link_of = lane % links
    quad_of = lane // links
    key = jnp.full((1, 4 * links), -1, i32)
    for a in range(atm_blocks):
        for l in range(link_total):
            slot = link_slot_in[a, l]
            used = l < link_count_in[a]
            read_slot[a * link_total + l] = jnp.where(used, slot, routes * capacity)
            row = (slot // capacity) * quad_rows + slot % capacity
            row = jnp.where(used, row, -quad_rows)
            key = jnp.where(link_of == a * link_total + l, row, key)
    key = key + quad_of * capacity
    key = jnp.where(key < 0, -1, key)
    row_of = lax.broadcasted_iota(i32, (routes * quad_rows, 4 * links), 0)
    slot_hits[...] = jnp.where(row_of == key, 1.0, 0.0).astype(bf16)

    lane = lax.broadcasted_iota(i32, (1, routes * flux_rows), 1)
    inner = lane % flux_rows
    slot_of = (lane // flux_rows) * capacity + inner % capacity
    key = jnp.full((1, routes * flux_rows), -1, i32)
    for o in range(3):
        for k in range(subs):
            for c in range(capacity):
                block = jnp.where(c < count_in[o, 0, k], block_in[0, o, k, c] * 16, -32)
                key = jnp.where(slot_of == (o * subs + k) * capacity + c, block, key)
    key = key + inner // capacity
    key = jnp.where(inner < fields_atm * capacity, key, -1)
    for part in range(4):
        rows = ocean_blocks * 4
        row_of = lax.broadcasted_iota(i32, (rows, routes * flux_rows), 0) + part * rows
        chooser[part * rows : (part + 1) * rows, :] = jnp.where(row_of == key, 1.0, 0.0).astype(
            bf16
        )
    row_of = lax.broadcasted_iota(i32, (fields_atm, fields_atm), 0)
    lane_of = lax.broadcasted_iota(i32, (fields_atm, fields_atm), 1)
    arrived[routes * capacity] = jnp.zeros((fields_ocean, width), f32)
    coefficient = []
    for f in range(fields_ocean):
        spread = jnp.where(row_of == lane_of, coupling_in[f : f + 1, :], 0.0)
        column = jnp.sum(spread, axis=1, keepdims=True)
        coefficient.append(jnp.broadcast_to(column, (fields_atm, width)))

    for copy in state_copies:
        copy.wait_recv()
    loads[9].wait()
    for p in range(routes):
        arrived[p * capacity : (p + 1) * capacity] = (
            state_recv[p].astype(f32).reshape(capacity, fields_ocean, width)
        )

    atm_acc = jnp.zeros((fields_atm, width), f32)
    for a in range(atm_blocks):
        taken = [arrived[read_slot[a * link_total + l]] for l in range(link_total)]
        taken = jnp.concatenate(taken, axis=1).astype(bf16)
        weight = weight_in[a].reshape(link_total * width, width)
        state_sum = jnp.dot(taken, weight, preferred_element_type=f32)
        here = slice(a * width, (a + 1) * width)
        state_out[:, here] = state_sum.astype(bf16)
        value = flux_in[:, here].astype(f32)
        change = coefficient[0] * state_sum[0:1]
        for f in range(1, fields_ocean):
            change = change + coefficient[f] * state_sum[f : f + 1]
        coupled = (value + change).astype(bf16)
        atm_acc = atm_acc + atm_area_in[a : a + 1, :] * coupled.astype(f32)
        part = lax.dot_general(
            coupled, weight, (((1,), (1,)), ((), ())), preferred_element_type=f32
        )
        for l in range(link_total):
            parts[pl.ds(a * link_total + l, fields_atm, stride=links), :] = part[
                :, l * width : (l + 1) * width
            ]

    quads = []
    for q in range(fields_atm // 4):
        operand = parts[q * 4 * links : (q + 1) * 4 * links, :].astype(bf16)
        quads.append(jnp.dot(slot_hits[...], operand, preferred_element_type=f32))
    blank = jnp.zeros((flux_rows - fields_atm * capacity, width), f32)
    for p in range(routes):
        rows = [quad[p * quad_rows : (p + 1) * quad_rows] for quad in quads]
        flux_send[p] = jnp.concatenate(rows + [blank], axis=0).astype(bf16)
    flux_copies = []
    for o, t in steps:
        copy = exchange(flux_send, flux_recv, flux_sems, o, t)
        copy.start()
        flux_copies.append(copy)
    flux_recv[subs + me_sub] = flux_send[subs + me_sub]

    for copy in area_copies:
        copy.wait_recv()
    ocean_acc = [jnp.zeros((quad_rows, width), f32) for _ in quads]
    for p in range(routes):
        area = area_recv[p][:capacity]
        area = jnp.concatenate([area] * 4, axis=0)
        for q, quad in enumerate(quads):
            rounded = quad[p * quad_rows : (p + 1) * quad_rows].astype(bf16).astype(f32)
            ocean_acc[q] = ocean_acc[q] + rounded * area

    def to_lanes(column, group):
        rows = column.shape[0]
        row_of = lax.broadcasted_iota(i32, (rows, 128), 0) // group
        lane_of = lax.broadcasted_iota(i32, (rows, 128), 1)
        return jnp.sum(jnp.where(row_of == lane_of, column, 0.0), axis=0, keepdims=True)

    ocean_rows = jnp.concatenate(ocean_acc, axis=0)
    mine = to_lanes(jnp.sum(atm_acc, axis=1, keepdims=True), 1) - to_lanes(
        jnp.sum(ocean_rows, axis=1, keepdims=True), capacity
    )
    sub_parts[me_sub] = mine
    sub_copies = []
    for t in range(1, subs):
        copy = pltpu.make_async_remote_copy(
            src_ref=sub_parts.at[me_sub],
            dst_ref=sub_parts.at[me_sub],
            send_sem=sub_sems.at[0, t],
            recv_sem=sub_sems.at[1, t],
            device_id=(me_grp, sub_at(t)),
            device_id_type=MESH,
        )
        copy.start()
        sub_copies.append(copy)
    for copy in sub_copies:
        copy.wait_recv()
    total = sub_parts[0]
    for k in range(1, subs):
        total = total + sub_parts[k]
    grp_parts[me_grp] = total
    grp_copies = []
    for d in range(1, groups):
        copy = pltpu.make_async_remote_copy(
            src_ref=grp_parts.at[me_grp],
            dst_ref=grp_parts.at[me_grp],
            send_sem=grp_sems.at[0, d],
            recv_sem=grp_sems.at[1, d],
            device_id=(grp_at(d), me_sub),
            device_id_type=MESH,
        )
        copy.start()
        grp_copies.append(copy)

    for copy in flux_copies:
        copy.wait_recv()
    returned = flux_recv[...].reshape(routes * flux_rows, width)
    flux_sum = jnp.dot(chooser[...], returned, preferred_element_type=f32)
    for b in range(ocean_blocks):
        flux_out[:, b * width : (b + 1) * width] = flux_sum[
            b * 16 : b * 16 + fields_atm
        ].astype(bf16)

    for copy in grp_copies:
        copy.wait_recv()
    total = grp_parts[0]
    for i in range(1, groups):
        total = total + grp_parts[i]
    imbalance_out[...] = total * norm_scale
    for copy in state_copies + area_copies + flux_copies + sub_copies + grp_copies:
        copy.wait_send()


def finish(state_in, flux_in, total_in, state_out, flux_out, total_out, sems):
    copies = [
        pltpu.make_async_copy(flux_in, flux_out, sems.at[0]),
        pltpu.make_async_copy(state_in, state_out, sems.at[1]),
    ]
    for copy in copies:
        copy.start()
    total_out[...] = total_in[0, : total_out.shape[0]]
    for copy in copies:
        copy.wait()


def shards(
    groups,
    subs,
    ocean_state,
    ocean_area,
    atm_flux,
    atm_area,
    coupling,
    remap_weight,
    send_block,
    send_count,
    link_slot,
    link_count,
):
    f32, bf16, i32 = jnp.float32, jnp.bfloat16, jnp.int32
    fields_ocean = ocean_state.shape[0]
    fields_atm = atm_flux.shape[0]
    atm_blocks, link_total, width = remap_weight.shape[:3]
    ocean_blocks = ocean_state.shape[1] // width
    capacity = send_block.shape[3]
    routes = 3 * subs
    links = atm_blocks * link_total
    flux_rows = -(-fields_atm * capacity // 16) * 16
    norm_scale = 1.0 / math.sqrt(groups * subs * atm_blocks * width)
    anywhere = pl.BlockSpec(memory_space=pl.ANY)
    vmem = pl.BlockSpec(memory_space=pltpu.VMEM)
    state_on_atm, flux_on_ocean, imbalance = pl.pallas_call(
        functools.partial(kernel, groups, subs, norm_scale),
        out_shape=(
            pltpu.VMEM((fields_ocean, atm_blocks * width), bf16),
            pltpu.VMEM((fields_atm, ocean_blocks * width), bf16),
            pltpu.VMEM((1, 128), f32),
        ),
        in_specs=[anywhere] * 10,
        out_specs=(vmem, vmem, vmem),
        scratch_shapes=[
            pltpu.VMEM(ocean_state.shape, bf16),
            pltpu.VMEM((ocean_blocks + 1, 1, width), f32),
            pltpu.VMEM(atm_flux.shape, bf16),
            pltpu.VMEM((atm_blocks, width), f32),
            pltpu.VMEM((fields_ocean, fields_atm), f32),
            pltpu.VMEM(remap_weight.shape, bf16),
            pltpu.SMEM(send_block.shape, i32),
            pltpu.SMEM((3, 1, subs), i32),
            pltpu.SMEM(link_slot.shape, i32),
            pltpu.SMEM(link_count.shape, i32),
            pltpu.SMEM((routes * capacity,), i32),
            pltpu.SMEM((links,), i32),
            pltpu.VMEM((ocean_blocks + 1, fields_ocean, width), f32),
            pltpu.VMEM((routes, capacity * fields_ocean, width), bf16),
            pltpu.VMEM((routes, capacity * fields_ocean, width), bf16),
            pltpu.VMEM((routes * capacity + 1, fields_ocean, width), f32),
            pltpu.VMEM((routes, 8, width), f32),
            pltpu.VMEM((routes, 8, width), f32),
            pltpu.VMEM((fields_atm * links, width), f32),
            pltpu.VMEM((routes * 4 * capacity, 4 * links), bf16),
            pltpu.VMEM((ocean_blocks * 16, routes * flux_rows), bf16),
            pltpu.VMEM((routes, flux_rows, width), bf16),
            pltpu.VMEM((routes, flux_rows, width), bf16),
            pltpu.VMEM((subs, 1, 128), f32),
            pltpu.VMEM((groups, 1, 128), f32),
            pltpu.SemaphoreType.DMA((10,)),
            pltpu.SemaphoreType.DMA((2, 3, subs)),
            pltpu.SemaphoreType.DMA((2, 3, subs)),
            pltpu.SemaphoreType.DMA((2, 3, subs)),
            pltpu.SemaphoreType.DMA((2, subs)),
            pltpu.SemaphoreType.DMA((2, groups)),
        ],
        compiler_params=pltpu.CompilerParams(
            collective_id=0, has_side_effects=True, vmem_limit_bytes=VMEM_BYTES
        ),
    )(
        ocean_state,
        ocean_area.reshape(ocean_blocks, 1, width),
        atm_flux,
        atm_area.reshape(atm_blocks, width),
        coupling.T,
        remap_weight,
        send_block,
        send_count.reshape(3, 1, subs),
        link_slot,
        link_count,
    )
    return pl.pallas_call(
        finish,
        out_shape=(
            jax.ShapeDtypeStruct(state_on_atm.shape, bf16),
            jax.ShapeDtypeStruct(flux_on_ocean.shape, bf16),
            jax.ShapeDtypeStruct((fields_atm,), f32),
        ),
        in_specs=[vmem, vmem, vmem],
        out_specs=(anywhere, anywhere, vmem),
        scratch_shapes=[pltpu.SemaphoreType.DMA((2,))],
        compiler_params=pltpu.CompilerParams(vmem_limit_bytes=1024 * 1024),
    )(state_on_atm, flux_on_ocean, imbalance)


def solution(mesh):
    placed = (
        P(None, ("grp", "sub")),
        P(("grp", "sub")),
        P(None, ("grp", "sub")),
        P(("grp", "sub")),
        P(),
        P(("grp", "sub"), None, None, None),
        P(("grp", "sub"), None, None, None),
        P(("grp", "sub"), None, None),
        P(("grp", "sub"), None),
        P(("grp", "sub")),
    )
    return jax.shard_map(
        functools.partial(shards, mesh.shape["grp"], mesh.shape["sub"]),
        mesh=mesh,
        in_specs=placed,
        out_specs=(P(None, ("grp", "sub")), P(None, ("grp", "sub")), P()),
        check_vma=False,
    )
```

```python
import functools
import math

import jax
import jax.numpy as jnp
from jax import lax
from jax.experimental import pallas as pl
from jax.experimental.pallas import tpu as pltpu
from jax.sharding import PartitionSpec as P

MESH = pl.DeviceIdType.MESH
VMEM_BYTES = 60 * 1024 * 1024


def kernel(
    groups,
    subs,
    norm_scale,
    state_hbm,
    ocean_area_hbm,
    flux_hbm,
    atm_area_hbm,
    coupling_hbm,
    weight_hbm,
    block_hbm,
    count_hbm,
    link_slot_hbm,
    link_count_hbm,
    state_out,
    flux_out,
    imbalance_out,
    state_in,
    ocean_area_in,
    flux_in,
    atm_area_in,
    coupling_in,
    weight_in,
    block_in,
    count_in,
    link_slot_in,
    link_count_in,
    picked,
    read_slot,
    state_wide,
    state_send,
    state_recv,
    arrived,
    area_send,
    area_recv,
    parts,
    slot_hits,
    chooser,
    flux_send,
    flux_recv,
    sub_parts,
    grp_parts,
    load_sem,
    state_sems,
    area_sems,
    flux_sems,
    sub_sems,
    grp_sems,
):
    f32, bf16, i32 = jnp.float32, jnp.bfloat16, jnp.int32
    ocean_blocks = ocean_area_hbm.shape[0]
    fields_ocean = state_wide.shape[1]
    width = state_wide.shape[2]
    fields_atm = flux_in.shape[0]
    atm_blocks, link_total = weight_in.shape[:2]
    capacity = block_in.shape[3]
    routes = 3 * subs
    links = atm_blocks * link_total
    quad_rows = 4 * capacity
    flux_rows = flux_send.shape[1]
    me_grp = lax.axis_index("grp")
    me_sub = lax.axis_index("sub")

    pairs = [
        (block_hbm, block_in),
        (count_hbm, count_in),
        (state_hbm, state_in),
        (ocean_area_hbm, ocean_area_in.at[pl.ds(0, ocean_area_hbm.shape[0])]),
        (link_slot_hbm, link_slot_in),
        (link_count_hbm, link_count_in),
        (coupling_hbm, coupling_in),
        (flux_hbm, flux_in),
        (atm_area_hbm, atm_area_in),
        (weight_hbm, weight_in),
    ]
    loads = [
        pltpu.make_async_copy(source, target, load_sem.at[n])
        for n, (source, target) in enumerate(pairs)
    ]
    for load in loads[:3]:
        load.start()

    steps = [(o, t) for o in (0, 2) for t in range(subs)] + [(1, t) for t in range(1, subs)]

    def grp_at(offset):
        return lax.rem(me_grp + offset + groups, groups)

    def sub_at(t):
        return lax.rem(me_sub + t, subs)

    barrier = pltpu.get_barrier_semaphore()
    partners = [(grp_at(o - 1), sub_at(t)) for o, t in steps]
    partners += [(grp_at(d), me_sub) for d in range(2, groups - 1)]
    for partner in partners:
        pl.semaphore_signal(barrier, inc=1, device_id=partner, device_id_type=MESH)

    for load in loads[3:]:
        load.start()

    def exchange(source, target, sems, o, t):
        k = sub_at(t)
        return pltpu.make_async_remote_copy(
            src_ref=source.at[o * subs + k],
            dst_ref=target.at[(2 - o) * subs + me_sub],
            send_sem=sems.at[0],
            recv_sem=sems.at[1],
            device_id=(grp_at(o - 1), k),
            device_id_type=MESH,
        )

    def drain(buffer, sem, count):
        ref = buffer.at[pl.ds(0, count)]
        pltpu.make_async_copy(ref, ref, sem).wait()

    loads[2].wait()
    for b in range(ocean_blocks):
        state_wide[b] = state_in[:, b * width : (b + 1) * width].astype(f32)
    state_wide[ocean_blocks] = jnp.zeros((fields_ocean, width), f32)

    loads[0].wait()
    loads[1].wait()

    def block_at(o, k, c):
        return jnp.where(c < count_in[o, 0, k], block_in[0, o, k, c], ocean_blocks)

    for o in range(3):
        for k in range(subs):
            for c in range(capacity):
                picked[(o * subs + k) * capacity + c] = block_at(o, k, c)

    for o in (0, 2, 1):
        for k in range(subs):
            first = (o * subs + k) * capacity
            rows = [state_wide[picked[first + c]] for c in range(capacity)]
            state_send[o * subs + k] = jnp.concatenate(rows, axis=0).astype(bf16)
        if o == 0:
            pl.semaphore_wait(barrier, len(partners))
        for t in range(1 if o == 1 else 0, subs):
            exchange(state_send, state_recv, state_sems, o, t).start()
    state_recv[subs + me_sub] = state_send[subs + me_sub]

    loads[3].wait()
    ocean_area_in[ocean_blocks] = jnp.zeros((1, width), f32)
    for o in (0, 2, 1):
        for k in range(subs):
            p = o * subs + k
            for c in range(capacity):
                area_send[p, c : c + 1, :] = ocean_area_in[picked[p * capacity + c]]
        for t in range(1 if o == 1 else 0, subs):
            exchange(area_send, area_recv, area_sems, o, t).start()
    area_recv[subs + me_sub] = area_send[subs + me_sub]

    for n in range(4, 9):
        loads[n].wait()
    lane = lax.broadcasted_iota(i32, (1, 4 * links), 1)
    link_of = lane % links
    quad_of = lane // links
    key = jnp.full((1, 4 * links), -1, i32)
    for a in range(atm_blocks):
        for l in range(link_total):
            slot = link_slot_in[a, l]
            used = l < link_count_in[a]
            read_slot[a * link_total + l] = jnp.where(used, slot, routes * capacity)
            row = (slot // capacity) * quad_rows + slot % capacity
            row = jnp.where(used, row, -quad_rows)
            key = jnp.where(link_of == a * link_total + l, row, key)
    key = key + quad_of * capacity
    key = jnp.where(key < 0, -1, key)
    row_of = lax.broadcasted_iota(i32, (routes * quad_rows, 4 * links), 0)
    slot_hits[...] = jnp.where(row_of == key, 1.0, 0.0).astype(bf16)

    row_of = lax.broadcasted_iota(i32, (16, fields_atm), 0)
    lane_of = lax.broadcasted_iota(i32, (16, fields_atm), 1)
    arrived[routes * capacity] = jnp.zeros((fields_ocean, width), f32)
    coefficient = []
    for f in range(fields_ocean):
        spread = jnp.where(row_of == lane_of, coupling_in[f : f + 1, :], 0.0)
        column = jnp.sum(spread, axis=1, keepdims=True)
        coefficient.append(jnp.broadcast_to(column, (16, width)))

    drain(state_recv, state_sems.at[1], len(steps))
    loads[9].wait()
    for p in range(routes):
        arrived[p * capacity : (p + 1) * capacity] = (
            state_recv[p].astype(f32).reshape(capacity, fields_ocean, width)
        )

    pairs = [(a, a + 1) for a in range(0, atm_blocks, 2)]

    def weight_of(pair):
        return jnp.concatenate(
            [weight_in[a].reshape(link_total * width, width) for a in pair], axis=1
        )

    sums = []
    for pair in pairs:
        taken = [
            jnp.concatenate([arrived[read_slot[a * link_total + l]] for a in pair], axis=0)
            for l in range(link_total)
        ]
        taken = jnp.concatenate(taken, axis=1).astype(bf16)
        both = jnp.dot(taken, weight_of(pair), preferred_element_type=f32)
        for n in range(2):
            sums.append(both[n * fields_ocean : (n + 1) * fields_ocean, n * width : (n + 1) * width])

    atm_acc = jnp.zeros((16, width), f32)
    margin = jnp.zeros((16 - fields_atm, width), f32)
    coupled = []
    for a, state_sum in enumerate(sums):
        here = slice(a * width, (a + 1) * width)
        state_out[:, here] = state_sum.astype(bf16)
        change = coefficient[0] * state_sum[0:1]
        for f in range(1, fields_ocean):
            change = change + coefficient[f] * state_sum[f : f + 1]
        value = jnp.concatenate([flux_in[:, here].astype(f32), margin], axis=0)
        coupled.append((value + change).astype(bf16))
        atm_acc = atm_acc + atm_area_in[a : a + 1, :] * coupled[a].astype(f32)

    none = jnp.zeros((16, width), bf16)
    for pair in pairs:
        left = jnp.concatenate([coupled[pair[0]], none], axis=0)
        right = jnp.concatenate([none, coupled[pair[1]]], axis=0)
        part = lax.dot_general(
            jnp.concatenate([left, right], axis=1),
            weight_of(pair),
            (((1,), (1,)), ((), ())),
            preferred_element_type=f32,
        )
        for n, a in enumerate(pair):
            for l in range(link_total):
                parts[pl.ds(a * link_total + l, fields_atm, stride=links), :] = part[
                    n * 16 : n * 16 + fields_atm, l * width : (l + 1) * width
                ]

    quads = []
    for q in range(fields_atm // 4):
        operand = parts[q * 4 * links : (q + 1) * 4 * links, :].astype(bf16)
        quads.append(jnp.dot(slot_hits[...], operand, preferred_element_type=f32))
    blank = jnp.zeros((flux_rows - fields_atm * capacity, width), f32)
    for p in range(routes):
        rows = [quad[p * quad_rows : (p + 1) * quad_rows] for quad in quads]
        flux_send[p] = jnp.concatenate(rows + [blank], axis=0).astype(bf16)
    for o, t in steps:
        exchange(flux_send, flux_recv, flux_sems, o, t).start()
    flux_recv[subs + me_sub] = flux_send[subs + me_sub]

    drain(area_recv, area_sems.at[1], len(steps))
    ocean_acc = [jnp.zeros((quad_rows, width), f32) for _ in quads]
    for p in range(routes):
        area = area_recv[p][:capacity]
        area = jnp.concatenate([area] * 4, axis=0)
        for q, quad in enumerate(quads):
            rounded = quad[p * quad_rows : (p + 1) * quad_rows].astype(bf16).astype(f32)
            ocean_acc[q] = ocean_acc[q] + rounded * area

    def to_lanes(column, group):
        rows = column.shape[0]
        row_of = lax.broadcasted_iota(i32, (rows, 128), 0) // group
        lane_of = lax.broadcasted_iota(i32, (rows, 128), 1)
        return jnp.sum(jnp.where(row_of == lane_of, column, 0.0), axis=0, keepdims=True)

    ocean_rows = jnp.concatenate(ocean_acc, axis=0)
    mine = to_lanes(jnp.sum(atm_acc, axis=1, keepdims=True), 1) - to_lanes(
        jnp.sum(ocean_rows, axis=1, keepdims=True), capacity
    )
    sub_parts[me_sub] = mine
    for t in range(1, subs):
        copy = pltpu.make_async_remote_copy(
            src_ref=sub_parts.at[me_sub],
            dst_ref=sub_parts.at[me_sub],
            send_sem=sub_sems.at[0],
            recv_sem=sub_sems.at[1],
            device_id=(me_grp, sub_at(t)),
            device_id_type=MESH,
        )
        copy.start()
    lane = lax.broadcasted_iota(i32, (1, routes * flux_rows), 1)
    inner = lane % flux_rows
    slot_of = (lane // flux_rows) * capacity + inner % capacity
    key = jnp.full((1, routes * flux_rows), -1, i32)
    for o in range(3):
        for k in range(subs):
            for c in range(capacity):
                block = jnp.where(c < count_in[o, 0, k], block_in[0, o, k, c] * 16, -32)
                key = jnp.where(slot_of == (o * subs + k) * capacity + c, block, key)
    key = key + inner // capacity
    key = jnp.where(inner < fields_atm * capacity, key, -1)
    for part in range(4):
        rows = ocean_blocks * 4
        row_of = lax.broadcasted_iota(i32, (rows, routes * flux_rows), 0) + part * rows
        chooser[part * rows : (part + 1) * rows, :] = jnp.where(row_of == key, 1.0, 0.0).astype(
            bf16
        )
    drain(sub_parts, sub_sems.at[1], subs - 1)
    total = sub_parts[0]
    for k in range(1, subs):
        total = total + sub_parts[k]
    grp_parts[me_grp] = total
    for d in range(1, groups):
        copy = pltpu.make_async_remote_copy(
            src_ref=grp_parts.at[me_grp],
            dst_ref=grp_parts.at[me_grp],
            send_sem=grp_sems.at[0],
            recv_sem=grp_sems.at[1],
            device_id=(grp_at(d), me_sub),
            device_id_type=MESH,
        )
        copy.start()
    drain(state_send, state_sems.at[0], len(steps))
    drain(area_send, area_sems.at[0], len(steps))
    drain(sub_parts, sub_sems.at[0], subs - 1)

    drain(flux_recv, flux_sems.at[1], len(steps))
    returned = flux_recv[...].reshape(routes * flux_rows, width)
    flux_sum = jnp.dot(chooser[...], returned, preferred_element_type=f32)
    for b in range(ocean_blocks):
        flux_out[:, b * width : (b + 1) * width] = flux_sum[
            b * 16 : b * 16 + fields_atm
        ].astype(bf16)

    drain(grp_parts, grp_sems.at[1], groups - 1)
    total = grp_parts[0]
    for i in range(1, groups):
        total = total + grp_parts[i]
    imbalance_out[...] = total * norm_scale
    drain(flux_send, flux_sems.at[0], len(steps))
    drain(grp_parts, grp_sems.at[0], groups - 1)


def finish(state_in, flux_in, total_in, state_out, flux_out, total_out, sems):
    copies = [
        pltpu.make_async_copy(flux_in, flux_out, sems.at[0]),
        pltpu.make_async_copy(state_in, state_out, sems.at[1]),
    ]
    for copy in copies:
        copy.start()
    total_out[...] = total_in[0, : total_out.shape[0]]
    for copy in copies:
        copy.wait()


def shards(
    groups,
    subs,
    ocean_state,
    ocean_area,
    atm_flux,
    atm_area,
    coupling,
    remap_weight,
    send_block,
    send_count,
    link_slot,
    link_count,
):
    f32, bf16, i32 = jnp.float32, jnp.bfloat16, jnp.int32
    fields_ocean = ocean_state.shape[0]
    fields_atm = atm_flux.shape[0]
    atm_blocks, link_total, width = remap_weight.shape[:3]
    ocean_blocks = ocean_state.shape[1] // width
    capacity = send_block.shape[3]
    routes = 3 * subs
    links = atm_blocks * link_total
    flux_rows = -(-fields_atm * capacity // 16) * 16
    norm_scale = 1.0 / math.sqrt(groups * subs * atm_blocks * width)
    anywhere = pl.BlockSpec(memory_space=pl.ANY)
    vmem = pl.BlockSpec(memory_space=pltpu.VMEM)
    state_on_atm, flux_on_ocean, imbalance = pl.pallas_call(
        functools.partial(kernel, groups, subs, norm_scale),
        out_shape=(
            pltpu.VMEM((fields_ocean, atm_blocks * width), bf16),
            pltpu.VMEM((fields_atm, ocean_blocks * width), bf16),
            pltpu.VMEM((1, 128), f32),
        ),
        in_specs=[anywhere] * 10,
        out_specs=(vmem, vmem, vmem),
        scratch_shapes=[
            pltpu.VMEM(ocean_state.shape, bf16),
            pltpu.VMEM((ocean_blocks + 1, 1, width), f32),
            pltpu.VMEM(atm_flux.shape, bf16),
            pltpu.VMEM((atm_blocks, width), f32),
            pltpu.VMEM((fields_ocean, fields_atm), f32),
            pltpu.VMEM(remap_weight.shape, bf16),
            pltpu.SMEM(send_block.shape, i32),
            pltpu.SMEM((3, 1, subs), i32),
            pltpu.SMEM(link_slot.shape, i32),
            pltpu.SMEM(link_count.shape, i32),
            pltpu.SMEM((routes * capacity,), i32),
            pltpu.SMEM((links,), i32),
            pltpu.VMEM((ocean_blocks + 1, fields_ocean, width), f32),
            pltpu.VMEM((routes, capacity * fields_ocean, width), bf16),
            pltpu.VMEM((routes, capacity * fields_ocean, width), bf16),
            pltpu.VMEM((routes * capacity + 1, fields_ocean, width), f32),
            pltpu.VMEM((routes, 8, width), f32),
            pltpu.VMEM((routes, 8, width), f32),
            pltpu.VMEM((fields_atm * links, width), f32),
            pltpu.VMEM((routes * 4 * capacity, 4 * links), bf16),
            pltpu.VMEM((ocean_blocks * 16, routes * flux_rows), bf16),
            pltpu.VMEM((routes, flux_rows, width), bf16),
            pltpu.VMEM((routes, flux_rows, width), bf16),
            pltpu.VMEM((subs, 1, 128), f32),
            pltpu.VMEM((groups, 1, 128), f32),
            pltpu.SemaphoreType.DMA((10,)),
            pltpu.SemaphoreType.DMA((2,)),
            pltpu.SemaphoreType.DMA((2,)),
            pltpu.SemaphoreType.DMA((2,)),
            pltpu.SemaphoreType.DMA((2,)),
            pltpu.SemaphoreType.DMA((2,)),
        ],
        compiler_params=pltpu.CompilerParams(
            collective_id=0, has_side_effects=True, vmem_limit_bytes=VMEM_BYTES
        ),
    )(
        ocean_state,
        ocean_area.reshape(ocean_blocks, 1, width),
        atm_flux,
        atm_area.reshape(atm_blocks, width),
        coupling.T,
        remap_weight,
        send_block,
        send_count.reshape(3, 1, subs),
        link_slot,
        link_count,
    )
    return pl.pallas_call(
        finish,
        out_shape=(
            jax.ShapeDtypeStruct(state_on_atm.shape, bf16),
            jax.ShapeDtypeStruct(flux_on_ocean.shape, bf16),
            jax.ShapeDtypeStruct((fields_atm,), f32),
        ),
        in_specs=[vmem, vmem, vmem],
        out_specs=(anywhere, anywhere, vmem),
        scratch_shapes=[pltpu.SemaphoreType.DMA((2,))],
        compiler_params=pltpu.CompilerParams(vmem_limit_bytes=1024 * 1024),
    )(state_on_atm, flux_on_ocean, imbalance)


def solution(mesh):
    placed = (
        P(None, ("grp", "sub")),
        P(("grp", "sub")),
        P(None, ("grp", "sub")),
        P(("grp", "sub")),
        P(),
        P(("grp", "sub"), None, None, None),
        P(("grp", "sub"), None, None, None),
        P(("grp", "sub"), None, None),
        P(("grp", "sub"), None),
        P(("grp", "sub")),
    )
    return jax.shard_map(
        functools.partial(shards, mesh.shape["grp"], mesh.shape["sub"]),
        mesh=mesh,
        in_specs=placed,
        out_specs=(P(None, ("grp", "sub")), P(None, ("grp", "sub")), P()),
        check_vma=False,
    )
```

```python
import functools
import math

import jax
import jax.numpy as jnp
from jax import lax
from jax.experimental import pallas as pl
from jax.experimental.pallas import tpu as pltpu
from jax.sharding import PartitionSpec as P

MESH = pl.DeviceIdType.MESH
VMEM_BYTES = 60 * 1024 * 1024


def kernel(
    groups,
    subs,
    norm_scale,
    state_hbm,
    ocean_area_hbm,
    flux_hbm,
    atm_area_hbm,
    coupling_hbm,
    weight_hbm,
    block_hbm,
    count_hbm,
    link_slot_hbm,
    link_count_hbm,
    state_out,
    returned_out,
    chooser,
    imbalance_out,
    state_in,
    ocean_area_in,
    flux_in,
    atm_area_in,
    coupling_in,
    weight_in,
    block_in,
    count_in,
    link_slot_in,
    link_count_in,
    picked,
    read_slot,
    state_wide,
    state_send,
    state_recv,
    arrived,
    area_send,
    area_recv,
    parts,
    slot_hits,
    flux_send,
    flux_recv,
    sub_parts,
    grp_parts,
    load_sem,
    state_sems,
    area_sems,
    flux_sems,
    sub_sems,
    grp_sems,
):
    f32, bf16, i32 = jnp.float32, jnp.bfloat16, jnp.int32
    ocean_blocks = ocean_area_hbm.shape[0]
    fields_ocean = state_wide.shape[1]
    width = state_wide.shape[2]
    fields_atm = flux_in.shape[0]
    atm_blocks, link_total = weight_in.shape[:2]
    capacity = block_in.shape[3]
    routes = 3 * subs
    links = atm_blocks * link_total
    pitch = links + 2
    quad_rows = 4 * capacity
    flux_rows = flux_send.shape[1]
    me_grp = lax.axis_index("grp")
    me_sub = lax.axis_index("sub")

    pairs = [
        (block_hbm, block_in),
        (count_hbm, count_in),
        (state_hbm, state_in),
        (ocean_area_hbm, ocean_area_in.at[pl.ds(0, ocean_area_hbm.shape[0])]),
        (link_slot_hbm, link_slot_in),
        (link_count_hbm, link_count_in),
        (coupling_hbm, coupling_in),
        (flux_hbm, flux_in),
        (atm_area_hbm, atm_area_in),
        (weight_hbm, weight_in),
    ]
    loads = [
        pltpu.make_async_copy(source, target, load_sem.at[n])
        for n, (source, target) in enumerate(pairs)
    ]
    for load in loads[:3]:
        load.start()

    steps = [(o, t) for o in (0, 2) for t in range(subs)] + [(1, t) for t in range(1, subs)]

    def grp_at(offset):
        return lax.rem(me_grp + offset + groups, groups)

    def sub_at(t):
        return lax.rem(me_sub + t, subs)

    barrier = pltpu.get_barrier_semaphore()
    partners = [(grp_at(o - 1), sub_at(t)) for o, t in steps]
    partners += [(grp_at(d), me_sub) for d in range(2, groups - 1)]
    for partner in partners:
        pl.semaphore_signal(barrier, inc=1, device_id=partner, device_id_type=MESH)

    for load in loads[3:]:
        load.start()

    def exchange(source, target, sems, o, t):
        k = sub_at(t)
        return pltpu.make_async_remote_copy(
            src_ref=source.at[o * subs + k],
            dst_ref=target.at[(2 - o) * subs + me_sub],
            send_sem=sems.at[0],
            recv_sem=sems.at[1],
            device_id=(grp_at(o - 1), k),
            device_id_type=MESH,
        )

    def drain(buffer, sem, count):
        ref = buffer.at[pl.ds(0, count)]
        pltpu.make_async_copy(ref, ref, sem).wait()

    loads[2].wait()
    for b in range(ocean_blocks):
        state_wide[b] = state_in[:, b * width : (b + 1) * width].astype(f32)
    state_wide[ocean_blocks] = jnp.zeros((fields_ocean, width), f32)

    loads[0].wait()
    loads[1].wait()

    def block_at(o, k, c):
        return jnp.where(c < count_in[o, 0, k], block_in[0, o, k, c], ocean_blocks)

    for o in range(3):
        for k in range(subs):
            for c in range(capacity):
                picked[(o * subs + k) * capacity + c] = block_at(o, k, c)

    for o in (0, 2, 1):
        for k in range(subs):
            first = (o * subs + k) * capacity
            rows = [state_wide[picked[first + c]] for c in range(capacity)]
            state_send[o * subs + k] = jnp.concatenate(rows, axis=0).astype(bf16)
        if o == 0:
            pl.semaphore_wait(barrier, len(partners))
        for t in range(1 if o == 1 else 0, subs):
            exchange(state_send, state_recv, state_sems, o, t).start()
    state_recv[subs + me_sub] = state_send[subs + me_sub]

    loads[3].wait()
    ocean_area_in[ocean_blocks] = jnp.zeros((1, width), f32)
    for o in (0, 2, 1):
        for k in range(subs):
            p = o * subs + k
            for c in range(capacity):
                area_send[p, c : c + 1, :] = ocean_area_in[picked[p * capacity + c]]
        for t in range(1 if o == 1 else 0, subs):
            exchange(area_send, area_recv, area_sems, o, t).start()
    area_recv[subs + me_sub] = area_send[subs + me_sub]

    for n in range(4, 9):
        loads[n].wait()
    lane = lax.broadcasted_iota(i32, (1, 4 * pitch), 1)
    link_of = lane % pitch
    quad_of = lane // pitch
    key = jnp.full((1, 4 * pitch), -quad_rows, i32)
    for a in range(atm_blocks):
        for l in range(link_total):
            slot = link_slot_in[a, l]
            used = l < link_count_in[a]
            read_slot[a * link_total + l] = jnp.where(used, slot, routes * capacity)
            row = (slot // capacity) * quad_rows + slot % capacity
            row = jnp.where(used, row, -quad_rows)
            key = jnp.where(link_of == a * link_total + l, row, key)
    key = key + quad_of * capacity
    key = jnp.where(key < 0, -1, key)
    row_of = lax.broadcasted_iota(i32, (routes * quad_rows, 4 * pitch), 0)
    slot_hits[...] = jnp.where(row_of == key, 1.0, 0.0).astype(bf16)

    row_of = lax.broadcasted_iota(i32, (16, fields_atm), 0)
    lane_of = lax.broadcasted_iota(i32, (16, fields_atm), 1)
    for g in range(fields_atm):
        parts[g * pitch + links : (g + 1) * pitch, :] = jnp.zeros((pitch - links, width), f32)
    arrived[routes * capacity] = jnp.zeros((fields_ocean, width), f32)
    coefficient = []
    for f in range(fields_ocean):
        spread = jnp.where(row_of == lane_of, coupling_in[f : f + 1, :], 0.0)
        column = jnp.sum(spread, axis=1, keepdims=True)
        coefficient.append(jnp.broadcast_to(column, (16, width)))

    drain(state_recv, state_sems.at[1], len(steps))
    loads[9].wait()
    for p in range(routes):
        arrived[p * capacity : (p + 1) * capacity] = (
            state_recv[p].astype(f32).reshape(capacity, fields_ocean, width)
        )

    pairs = [(a, a + 1) for a in range(0, atm_blocks, 2)]

    def weight_of(pair):
        return jnp.concatenate(
            [weight_in[a].reshape(link_total * width, width) for a in pair], axis=1
        )

    sums = []
    for pair in pairs:
        taken = [
            jnp.concatenate([arrived[read_slot[a * link_total + l]] for a in pair], axis=0)
            for l in range(link_total)
        ]
        taken = jnp.concatenate(taken, axis=1).astype(bf16)
        both = jnp.dot(taken, weight_of(pair), preferred_element_type=f32)
        for n in range(2):
            sums.append(both[n * fields_ocean : (n + 1) * fields_ocean, n * width : (n + 1) * width])

    atm_acc = jnp.zeros((16, width), f32)
    margin = jnp.zeros((16 - fields_atm, width), f32)
    coupled = []
    for a, state_sum in enumerate(sums):
        here = slice(a * width, (a + 1) * width)
        state_out[:, here] = state_sum.astype(bf16)
        change = coefficient[0] * state_sum[0:1]
        for f in range(1, fields_ocean):
            change = change + coefficient[f] * state_sum[f : f + 1]
        value = jnp.concatenate([flux_in[:, here].astype(f32), margin], axis=0)
        coupled.append((value + change).astype(bf16))
        atm_acc = atm_acc + atm_area_in[a : a + 1, :] * coupled[a].astype(f32)

    none = jnp.zeros((16, width), bf16)
    for pair in pairs:
        left = jnp.concatenate([coupled[pair[0]], none], axis=0)
        right = jnp.concatenate([none, coupled[pair[1]]], axis=0)
        part = lax.dot_general(
            jnp.concatenate([left, right], axis=1),
            weight_of(pair),
            (((1,), (1,)), ((), ())),
            preferred_element_type=f32,
        )
        for n, a in enumerate(pair):
            for l in range(link_total):
                parts[pl.ds(a * link_total + l, fields_atm, stride=pitch), :] = part[
                    n * 16 : n * 16 + fields_atm, l * width : (l + 1) * width
                ]

    quads = []
    for q in range(fields_atm // 4):
        operand = parts[q * 4 * pitch : (q + 1) * 4 * pitch, :].astype(bf16)
        quads.append(jnp.dot(slot_hits[...], operand, preferred_element_type=f32))
    blank = jnp.zeros((flux_rows - fields_atm * capacity, width), f32)
    for p in range(routes):
        rows = [quad[p * quad_rows : (p + 1) * quad_rows] for quad in quads]
        flux_send[p] = jnp.concatenate(rows + [blank], axis=0).astype(bf16)
    for o, t in steps:
        exchange(flux_send, flux_recv, flux_sems, o, t).start()
    flux_recv[subs + me_sub] = flux_send[subs + me_sub]

    drain(area_recv, area_sems.at[1], len(steps))
    ocean_acc = [jnp.zeros((quad_rows, width), f32) for _ in quads]
    for p in range(routes):
        area = area_recv[p][:capacity]
        area = jnp.concatenate([area] * 4, axis=0)
        for q, quad in enumerate(quads):
            rounded = quad[p * quad_rows : (p + 1) * quad_rows].astype(bf16).astype(f32)
            ocean_acc[q] = ocean_acc[q] + rounded * area

    def to_lanes(column, group):
        rows = column.shape[0]
        row_of = lax.broadcasted_iota(i32, (rows, 128), 0) // group
        lane_of = lax.broadcasted_iota(i32, (rows, 128), 1)
        return jnp.sum(jnp.where(row_of == lane_of, column, 0.0), axis=0, keepdims=True)

    ocean_rows = jnp.concatenate(ocean_acc, axis=0)
    mine = to_lanes(jnp.sum(atm_acc, axis=1, keepdims=True), 1) - to_lanes(
        jnp.sum(ocean_rows, axis=1, keepdims=True), capacity
    )
    sub_parts[me_sub] = mine
    for t in range(1, subs):
        copy = pltpu.make_async_remote_copy(
            src_ref=sub_parts.at[me_sub],
            dst_ref=sub_parts.at[me_sub],
            send_sem=sub_sems.at[0],
            recv_sem=sub_sems.at[1],
            device_id=(me_grp, sub_at(t)),
            device_id_type=MESH,
        )
        copy.start()
    lane = lax.broadcasted_iota(i32, (1, routes * flux_rows), 1)
    inner = lane % flux_rows
    slot_of = (lane // flux_rows) * capacity + inner % capacity
    key = jnp.full((1, routes * flux_rows), -1, i32)
    for o in range(3):
        for k in range(subs):
            for c in range(capacity):
                block = jnp.where(c < count_in[o, 0, k], block_in[0, o, k, c] * 16, -32)
                key = jnp.where(slot_of == (o * subs + k) * capacity + c, block, key)
    key = key + inner // capacity
    key = jnp.where(inner < fields_atm * capacity, key, -1)
    for part in range(4):
        rows = ocean_blocks * 4
        row_of = lax.broadcasted_iota(i32, (rows, routes * flux_rows), 0) + part * rows
        chooser[part * rows : (part + 1) * rows, :] = jnp.where(row_of == key, 1.0, 0.0).astype(
            bf16
        )
    drain(sub_parts, sub_sems.at[1], subs - 1)
    total = sub_parts[0]
    for k in range(1, subs):
        total = total + sub_parts[k]
    grp_parts[me_grp] = total
    for d in range(1, groups):
        copy = pltpu.make_async_remote_copy(
            src_ref=grp_parts.at[me_grp],
            dst_ref=grp_parts.at[me_grp],
            send_sem=grp_sems.at[0],
            recv_sem=grp_sems.at[1],
            device_id=(grp_at(d), me_sub),
            device_id_type=MESH,
        )
        copy.start()
    drain(state_send, state_sems.at[0], len(steps))
    drain(area_send, area_sems.at[0], len(steps))
    drain(sub_parts, sub_sems.at[0], subs - 1)

    drain(flux_recv, flux_sems.at[1], len(steps))
    returned_out[...] = flux_recv[...].reshape(routes * flux_rows, width)

    drain(grp_parts, grp_sems.at[1], groups - 1)
    total = grp_parts[0]
    for i in range(1, groups):
        total = total + grp_parts[i]
    imbalance_out[...] = total * norm_scale
    drain(flux_send, flux_sems.at[0], len(steps))
    drain(grp_parts, grp_sems.at[0], groups - 1)


def finish(
    state_in, returned, chooser, total_in, state_out, flux_out, total_out, flux_sum, sems
):
    width = returned.shape[1]
    fields_atm = flux_sum.shape[0]
    store_state = pltpu.make_async_copy(state_in, state_out, sems.at[2])
    store_state.start()
    half = chooser.shape[0] // 2
    blocks = half // 16
    stores = []
    for n in range(2):
        block_sum = jnp.dot(
            chooser[n * half : (n + 1) * half, :],
            returned[...],
            preferred_element_type=jnp.float32,
        )
        for b in range(blocks):
            at = (n * blocks + b) * width
            flux_sum[:, at : at + width] = block_sum[b * 16 : b * 16 + fields_atm].astype(
                jnp.bfloat16
            )
        part = pl.ds(n * blocks * width, blocks * width)
        store = pltpu.make_async_copy(flux_sum.at[:, part], flux_out.at[:, part], sems.at[n])
        store.start()
        stores.append(store)
    total_out[...] = total_in[0, : total_out.shape[0]]
    for store in stores + [store_state]:
        store.wait()


def shards(
    groups,
    subs,
    ocean_state,
    ocean_area,
    atm_flux,
    atm_area,
    coupling,
    remap_weight,
    send_block,
    send_count,
    link_slot,
    link_count,
):
    f32, bf16, i32 = jnp.float32, jnp.bfloat16, jnp.int32
    fields_ocean = ocean_state.shape[0]
    fields_atm = atm_flux.shape[0]
    atm_blocks, link_total, width = remap_weight.shape[:3]
    ocean_blocks = ocean_state.shape[1] // width
    capacity = send_block.shape[3]
    routes = 3 * subs
    links = atm_blocks * link_total
    pitch = links + 2
    flux_rows = -(-fields_atm * capacity // 16) * 16
    norm_scale = 1.0 / math.sqrt(groups * subs * atm_blocks * width)
    anywhere = pl.BlockSpec(memory_space=pl.ANY)
    vmem = pl.BlockSpec(memory_space=pltpu.VMEM)
    state_on_atm, returned, chooser, imbalance = pl.pallas_call(
        functools.partial(kernel, groups, subs, norm_scale),
        out_shape=(
            pltpu.VMEM((fields_ocean, atm_blocks * width), bf16),
            pltpu.VMEM((routes * flux_rows, width), bf16),
            pltpu.VMEM((ocean_blocks * 16, routes * flux_rows), bf16),
            pltpu.VMEM((1, 128), f32),
        ),
        in_specs=[anywhere] * 10,
        out_specs=(vmem, vmem, vmem, vmem),
        scratch_shapes=[
            pltpu.VMEM(ocean_state.shape, bf16),
            pltpu.VMEM((ocean_blocks + 1, 1, width), f32),
            pltpu.VMEM(atm_flux.shape, bf16),
            pltpu.VMEM((atm_blocks, width), f32),
            pltpu.VMEM((fields_ocean, fields_atm), f32),
            pltpu.VMEM(remap_weight.shape, bf16),
            pltpu.SMEM(send_block.shape, i32),
            pltpu.SMEM((3, 1, subs), i32),
            pltpu.SMEM(link_slot.shape, i32),
            pltpu.SMEM(link_count.shape, i32),
            pltpu.SMEM((routes * capacity,), i32),
            pltpu.SMEM((links,), i32),
            pltpu.VMEM((ocean_blocks + 1, fields_ocean, width), f32),
            pltpu.VMEM((routes, capacity * fields_ocean, width), bf16),
            pltpu.VMEM((routes, capacity * fields_ocean, width), bf16),
            pltpu.VMEM((routes * capacity + 1, fields_ocean, width), f32),
            pltpu.VMEM((routes, 8, width), f32),
            pltpu.VMEM((routes, 8, width), f32),
            pltpu.VMEM((fields_atm * pitch, width), f32),
            pltpu.VMEM((routes * 4 * capacity, 4 * pitch), bf16),
            pltpu.VMEM((routes, flux_rows, width), bf16),
            pltpu.VMEM((routes, flux_rows, width), bf16),
            pltpu.VMEM((subs, 1, 128), f32),
            pltpu.VMEM((groups, 1, 128), f32),
            pltpu.SemaphoreType.DMA((10,)),
            pltpu.SemaphoreType.DMA((2,)),
            pltpu.SemaphoreType.DMA((2,)),
            pltpu.SemaphoreType.DMA((2,)),
            pltpu.SemaphoreType.DMA((2,)),
            pltpu.SemaphoreType.DMA((2,)),
        ],
        compiler_params=pltpu.CompilerParams(
            collective_id=0, has_side_effects=True, vmem_limit_bytes=VMEM_BYTES
        ),
    )(
        ocean_state,
        ocean_area.reshape(ocean_blocks, 1, width),
        atm_flux,
        atm_area.reshape(atm_blocks, width),
        coupling.T,
        remap_weight,
        send_block,
        send_count.reshape(3, 1, subs),
        link_slot,
        link_count,
    )
    return pl.pallas_call(
        finish,
        out_shape=(
            jax.ShapeDtypeStruct(state_on_atm.shape, bf16),
            jax.ShapeDtypeStruct((fields_atm, ocean_blocks * width), bf16),
            jax.ShapeDtypeStruct((fields_atm,), f32),
        ),
        in_specs=[vmem] * 4,
        out_specs=(anywhere, anywhere, vmem),
        scratch_shapes=[
            pltpu.VMEM((fields_atm, ocean_blocks * width), bf16),
            pltpu.SemaphoreType.DMA((3,)),
        ],
        compiler_params=pltpu.CompilerParams(vmem_limit_bytes=8 * 1024 * 1024),
    )(state_on_atm, returned, chooser, imbalance)


def solution(mesh):
    placed = (
        P(None, ("grp", "sub")),
        P(("grp", "sub")),
        P(None, ("grp", "sub")),
        P(("grp", "sub")),
        P(),
        P(("grp", "sub"), None, None, None),
        P(("grp", "sub"), None, None, None),
        P(("grp", "sub"), None, None),
        P(("grp", "sub"), None),
        P(("grp", "sub")),
    )
    return jax.shard_map(
        functools.partial(shards, mesh.shape["grp"], mesh.shape["sub"]),
        mesh=mesh,
        in_specs=placed,
        out_specs=(P(None, ("grp", "sub")), P(None, ("grp", "sub")), P()),
        check_vma=False,
    )
```

```python
import functools
import math

import jax
import jax.numpy as jnp
from jax import lax
from jax.experimental import pallas as pl
from jax.experimental.pallas import tpu as pltpu
from jax.sharding import PartitionSpec as P

MESH = pl.DeviceIdType.MESH
VMEM_BYTES = 60 * 1024 * 1024


def kernel(
    groups,
    subs,
    norm_scale,
    state_hbm,
    ocean_area_hbm,
    flux_hbm,
    atm_area_hbm,
    coupling_hbm,
    weight_hbm,
    block_hbm,
    count_hbm,
    link_slot_hbm,
    link_count_hbm,
    state_out,
    flux_out,
    imbalance_out,
    state_in,
    ocean_area_in,
    flux_in,
    atm_area_in,
    coupling_in,
    weight_in,
    block_in,
    count_in,
    link_slot_in,
    link_count_in,
    picked,
    read_slot,
    state_wide,
    state_send,
    state_recv,
    arrived,
    area_send,
    area_recv,
    parts,
    slot_hits,
    chooser,
    flux_send,
    flux_recv,
    totals,
    load_sem,
    state_sems,
    area_sems,
    flux_sems,
    total_sems,
):
    f32, bf16, i32 = jnp.float32, jnp.bfloat16, jnp.int32
    ocean_blocks = ocean_area_hbm.shape[0]
    fields_ocean = state_wide.shape[1]
    width = state_wide.shape[2]
    fields_atm = flux_in.shape[0]
    atm_blocks, link_total = weight_in.shape[:2]
    capacity = block_in.shape[3]
    routes = 3 * subs
    links = atm_blocks * link_total
    quad_rows = 4 * capacity
    flux_rows = flux_send.shape[1]
    me_grp = lax.axis_index("grp")
    me_sub = lax.axis_index("sub")

    pairs = [
        (block_hbm, block_in),
        (count_hbm, count_in),
        (state_hbm, state_in),
        (ocean_area_hbm, ocean_area_in.at[pl.ds(0, ocean_area_hbm.shape[0])]),
        (link_slot_hbm, link_slot_in),
        (link_count_hbm, link_count_in),
        (coupling_hbm, coupling_in),
        (flux_hbm, flux_in),
        (atm_area_hbm, atm_area_in),
        (weight_hbm, weight_in),
    ]
    loads = [
        pltpu.make_async_copy(source, target, load_sem.at[n])
        for n, (source, target) in enumerate(pairs)
    ]
    for load in loads[:3]:
        load.start()

    steps = [(o, t) for o in (0, 2) for t in range(subs)] + [(1, t) for t in range(1, subs)]

    def grp_at(offset):
        return lax.rem(me_grp + offset + groups, groups)

    def sub_at(t):
        return lax.rem(me_sub + t, subs)

    barrier = pltpu.get_barrier_semaphore()
    others = groups * subs - 1

    def each_other(visit):
        def body(n, carry):
            visit((grp_at(n // subs), sub_at(n % subs)))
            return carry

        lax.fori_loop(1, others + 1, body, 0, unroll=others < 64)

    def greet(partner):
        pl.semaphore_signal(barrier, inc=1, device_id=partner, device_id_type=MESH)

    each_other(greet)

    for load in loads[3:]:
        load.start()

    def exchange(source, target, sems, o, t):
        k = sub_at(t)
        return pltpu.make_async_remote_copy(
            src_ref=source.at[o * subs + k],
            dst_ref=target.at[(2 - o) * subs + me_sub],
            send_sem=sems.at[0],
            recv_sem=sems.at[1],
            device_id=(grp_at(o - 1), k),
            device_id_type=MESH,
        )

    def drain(buffer, sem, count):
        ref = buffer.at[pl.ds(0, count)]
        pltpu.make_async_copy(ref, ref, sem).wait()

    loads[2].wait()
    for b in range(ocean_blocks):
        state_wide[b] = state_in[:, b * width : (b + 1) * width].astype(f32)
    state_wide[ocean_blocks] = jnp.zeros((fields_ocean, width), f32)

    loads[0].wait()
    loads[1].wait()

    def block_at(o, k, c):
        return jnp.where(c < count_in[o, 0, k], block_in[0, o, k, c], ocean_blocks)

    for o in range(3):
        for k in range(subs):
            for c in range(capacity):
                picked[(o * subs + k) * capacity + c] = block_at(o, k, c)

    for o in (0, 2, 1):
        for k in range(subs):
            first = (o * subs + k) * capacity
            rows = [state_wide[picked[first + c]] for c in range(capacity)]
            state_send[o * subs + k] = jnp.concatenate(rows, axis=0).astype(bf16)
        if o == 0:
            pl.semaphore_wait(barrier, others)
        for t in range(1 if o == 1 else 0, subs):
            exchange(state_send, state_recv, state_sems, o, t).start()
    state_recv[subs + me_sub] = state_send[subs + me_sub]

    loads[3].wait()
    ocean_area_in[ocean_blocks] = jnp.zeros((1, width), f32)
    for o in (0, 2, 1):
        for k in range(subs):
            p = o * subs + k
            for c in range(capacity):
                area_send[p, c : c + 1, :] = ocean_area_in[picked[p * capacity + c]]
        for t in range(1 if o == 1 else 0, subs):
            exchange(area_send, area_recv, area_sems, o, t).start()
    area_recv[subs + me_sub] = area_send[subs + me_sub]

    for n in range(4, 9):
        loads[n].wait()
    lane = lax.broadcasted_iota(i32, (1, 4 * links), 1)
    link_of = lane % links
    quad_of = lane // links
    key = jnp.full((1, 4 * links), -1, i32)
    for a in range(atm_blocks):
        for l in range(link_total):
            slot = link_slot_in[a, l]
            used = l < link_count_in[a]
            read_slot[a * link_total + l] = jnp.where(used, slot, routes * capacity)
            row = (slot // capacity) * quad_rows + slot % capacity
            row = jnp.where(used, row, -quad_rows)
            key = jnp.where(link_of == a * link_total + l, row, key)
    key = key + quad_of * capacity
    key = jnp.where(key < 0, -1, key)
    row_of = lax.broadcasted_iota(i32, (routes * quad_rows, 4 * links), 0)
    slot_hits[...] = jnp.where(row_of == key, 1.0, 0.0).astype(bf16)

    row_of = lax.broadcasted_iota(i32, (16, fields_atm), 0)
    lane_of = lax.broadcasted_iota(i32, (16, fields_atm), 1)
    arrived[routes * capacity] = jnp.zeros((fields_ocean, width), f32)
    coefficient = []
    for f in range(fields_ocean):
        spread = jnp.where(row_of == lane_of, coupling_in[f : f + 1, :], 0.0)
        column = jnp.sum(spread, axis=1, keepdims=True)
        coefficient.append(jnp.broadcast_to(column, (16, width)))

    drain(state_recv, state_sems.at[1], len(steps))
    loads[9].wait()
    for p in range(routes):
        arrived[p * capacity : (p + 1) * capacity] = (
            state_recv[p].astype(f32).reshape(capacity, fields_ocean, width)
        )

    pairs = [(a, a + 1) for a in range(0, atm_blocks, 2)]

    def weight_of(pair):
        return jnp.concatenate(
            [weight_in[a].reshape(link_total * width, width) for a in pair], axis=1
        )

    sums = []
    for pair in pairs:
        taken = [
            jnp.concatenate([arrived[read_slot[a * link_total + l]] for a in pair], axis=0)
            for l in range(link_total)
        ]
        taken = jnp.concatenate(taken, axis=1).astype(bf16)
        both = jnp.dot(taken, weight_of(pair), preferred_element_type=f32)
        for n in range(2):
            sums.append(both[n * fields_ocean : (n + 1) * fields_ocean, n * width : (n + 1) * width])

    atm_acc = jnp.zeros((16, width), f32)
    margin = jnp.zeros((16 - fields_atm, width), f32)
    coupled = []
    for a, state_sum in enumerate(sums):
        here = slice(a * width, (a + 1) * width)
        state_out[:, here] = state_sum.astype(bf16)
        change = coefficient[0] * state_sum[0:1]
        for f in range(1, fields_ocean):
            change = change + coefficient[f] * state_sum[f : f + 1]
        value = jnp.concatenate([flux_in[:, here].astype(f32), margin], axis=0)
        coupled.append((value + change).astype(bf16))
        atm_acc = atm_acc + atm_area_in[a : a + 1, :] * coupled[a].astype(f32)

    none = jnp.zeros((16, width), bf16)
    for pair in pairs:
        left = jnp.concatenate([coupled[pair[0]], none], axis=0)
        right = jnp.concatenate([none, coupled[pair[1]]], axis=0)
        part = lax.dot_general(
            jnp.concatenate([left, right], axis=1),
            weight_of(pair),
            (((1,), (1,)), ((), ())),
            preferred_element_type=f32,
        )
        for n, a in enumerate(pair):
            for l in range(link_total):
                parts[pl.ds(a * link_total + l, fields_atm, stride=links), :] = part[
                    n * 16 : n * 16 + fields_atm, l * width : (l + 1) * width
                ]

    quads = []
    for q in range(fields_atm // 4):
        operand = parts[q * 4 * links : (q + 1) * 4 * links, :].astype(bf16)
        quads.append(jnp.dot(slot_hits[...], operand, preferred_element_type=f32))
    blank = jnp.zeros((flux_rows - fields_atm * capacity, width), f32)
    for p in range(routes):
        rows = [quad[p * quad_rows : (p + 1) * quad_rows] for quad in quads]
        flux_send[p] = jnp.concatenate(rows + [blank], axis=0).astype(bf16)
    for o, t in steps:
        exchange(flux_send, flux_recv, flux_sems, o, t).start()
    flux_recv[subs + me_sub] = flux_send[subs + me_sub]

    drain(area_recv, area_sems.at[1], len(steps))
    ocean_acc = [jnp.zeros((quad_rows, width), f32) for _ in quads]
    for p in range(routes):
        area = area_recv[p][:capacity]
        area = jnp.concatenate([area] * 4, axis=0)
        for q, quad in enumerate(quads):
            rounded = quad[p * quad_rows : (p + 1) * quad_rows].astype(bf16).astype(f32)
            ocean_acc[q] = ocean_acc[q] + rounded * area

    def to_lanes(column, group):
        rows = column.shape[0]
        row_of = lax.broadcasted_iota(i32, (rows, 128), 0) // group
        lane_of = lax.broadcasted_iota(i32, (rows, 128), 1)
        return jnp.sum(jnp.where(row_of == lane_of, column, 0.0), axis=0, keepdims=True)

    ocean_rows = jnp.concatenate(ocean_acc, axis=0)
    mine = to_lanes(jnp.sum(atm_acc, axis=1, keepdims=True), 1) - to_lanes(
        jnp.sum(ocean_rows, axis=1, keepdims=True), capacity
    )
    me = me_grp * subs + me_sub
    totals[me] = mine

    def tell(partner):
        pltpu.make_async_remote_copy(
            src_ref=totals.at[me],
            dst_ref=totals.at[me],
            send_sem=total_sems.at[0],
            recv_sem=total_sems.at[1],
            device_id=partner,
            device_id_type=MESH,
        ).start()

    each_other(tell)
    lane = lax.broadcasted_iota(i32, (1, routes * flux_rows), 1)
    inner = lane % flux_rows
    slot_of = (lane // flux_rows) * capacity + inner % capacity
    key = jnp.full((1, routes * flux_rows), -1, i32)
    for o in range(3):
        for k in range(subs):
            for c in range(capacity):
                block = jnp.where(c < count_in[o, 0, k], block_in[0, o, k, c] * 16, -32)
                key = jnp.where(slot_of == (o * subs + k) * capacity + c, block, key)
    key = key + inner // capacity
    key = jnp.where(inner < fields_atm * capacity, key, -1)
    for part in range(4):
        rows = ocean_blocks * 4
        row_of = lax.broadcasted_iota(i32, (rows, routes * flux_rows), 0) + part * rows
        chooser[part * rows : (part + 1) * rows, :] = jnp.where(row_of == key, 1.0, 0.0).astype(
            bf16
        )
    drain(state_send, state_sems.at[0], len(steps))
    drain(area_send, area_sems.at[0], len(steps))

    drain(flux_recv, flux_sems.at[1], len(steps))
    returned = flux_recv[...].reshape(routes * flux_rows, width)
    flux_sum = jnp.dot(chooser[...], returned, preferred_element_type=f32)
    for b in range(ocean_blocks):
        flux_out[:, b * width : (b + 1) * width] = flux_sum[
            b * 16 : b * 16 + fields_atm
        ].astype(bf16)

    drain(totals, total_sems.at[1], others)
    imbalance_out[...] = jnp.sum(totals[...], axis=0) * norm_scale
    drain(flux_send, flux_sems.at[0], len(steps))
    drain(totals, total_sems.at[0], others)


def finish(state_in, flux_in, total_in, state_out, flux_out, total_out, sems):
    copies = [
        pltpu.make_async_copy(flux_in, flux_out, sems.at[0]),
        pltpu.make_async_copy(state_in, state_out, sems.at[1]),
    ]
    for copy in copies:
        copy.start()
    total_out[...] = total_in[0, : total_out.shape[0]]
    for copy in copies:
        copy.wait()


def shards(
    groups,
    subs,
    ocean_state,
    ocean_area,
    atm_flux,
    atm_area,
    coupling,
    remap_weight,
    send_block,
    send_count,
    link_slot,
    link_count,
):
    f32, bf16, i32 = jnp.float32, jnp.bfloat16, jnp.int32
    fields_ocean = ocean_state.shape[0]
    fields_atm = atm_flux.shape[0]
    atm_blocks, link_total, width = remap_weight.shape[:3]
    ocean_blocks = ocean_state.shape[1] // width
    capacity = send_block.shape[3]
    routes = 3 * subs
    links = atm_blocks * link_total
    flux_rows = -(-fields_atm * capacity // 16) * 16
    norm_scale = 1.0 / math.sqrt(groups * subs * atm_blocks * width)
    anywhere = pl.BlockSpec(memory_space=pl.ANY)
    vmem = pl.BlockSpec(memory_space=pltpu.VMEM)
    state_on_atm, flux_on_ocean, imbalance = pl.pallas_call(
        functools.partial(kernel, groups, subs, norm_scale),
        out_shape=(
            pltpu.VMEM((fields_ocean, atm_blocks * width), bf16),
            pltpu.VMEM((fields_atm, ocean_blocks * width), bf16),
            pltpu.VMEM((1, 128), f32),
        ),
        in_specs=[anywhere] * 10,
        out_specs=(vmem, vmem, vmem),
        scratch_shapes=[
            pltpu.VMEM(ocean_state.shape, bf16),
            pltpu.VMEM((ocean_blocks + 1, 1, width), f32),
            pltpu.VMEM(atm_flux.shape, bf16),
            pltpu.VMEM((atm_blocks, width), f32),
            pltpu.VMEM((fields_ocean, fields_atm), f32),
            pltpu.VMEM(remap_weight.shape, bf16),
            pltpu.SMEM(send_block.shape, i32),
            pltpu.SMEM((3, 1, subs), i32),
            pltpu.SMEM(link_slot.shape, i32),
            pltpu.SMEM(link_count.shape, i32),
            pltpu.SMEM((routes * capacity,), i32),
            pltpu.SMEM((links,), i32),
            pltpu.VMEM((ocean_blocks + 1, fields_ocean, width), f32),
            pltpu.VMEM((routes, capacity * fields_ocean, width), bf16),
            pltpu.VMEM((routes, capacity * fields_ocean, width), bf16),
            pltpu.VMEM((routes * capacity + 1, fields_ocean, width), f32),
            pltpu.VMEM((routes, 8, width), f32),
            pltpu.VMEM((routes, 8, width), f32),
            pltpu.VMEM((fields_atm * links, width), f32),
            pltpu.VMEM((routes * 4 * capacity, 4 * links), bf16),
            pltpu.VMEM((ocean_blocks * 16, routes * flux_rows), bf16),
            pltpu.VMEM((routes, flux_rows, width), bf16),
            pltpu.VMEM((routes, flux_rows, width), bf16),
            pltpu.VMEM((groups * subs, 1, 128), f32),
            pltpu.SemaphoreType.DMA((10,)),
            pltpu.SemaphoreType.DMA((2,)),
            pltpu.SemaphoreType.DMA((2,)),
            pltpu.SemaphoreType.DMA((2,)),
            pltpu.SemaphoreType.DMA((2,)),
        ],
        compiler_params=pltpu.CompilerParams(
            collective_id=0, has_side_effects=True, vmem_limit_bytes=VMEM_BYTES
        ),
    )(
        ocean_state,
        ocean_area.reshape(ocean_blocks, 1, width),
        atm_flux,
        atm_area.reshape(atm_blocks, width),
        coupling.T,
        remap_weight,
        send_block,
        send_count.reshape(3, 1, subs),
        link_slot,
        link_count,
    )
    return pl.pallas_call(
        finish,
        out_shape=(
            jax.ShapeDtypeStruct(state_on_atm.shape, bf16),
            jax.ShapeDtypeStruct(flux_on_ocean.shape, bf16),
            jax.ShapeDtypeStruct((fields_atm,), f32),
        ),
        in_specs=[vmem, vmem, vmem],
        out_specs=(anywhere, anywhere, vmem),
        scratch_shapes=[pltpu.SemaphoreType.DMA((2,))],
        compiler_params=pltpu.CompilerParams(vmem_limit_bytes=1024 * 1024),
    )(state_on_atm, flux_on_ocean, imbalance)


def solution(mesh):
    placed = (
        P(None, ("grp", "sub")),
        P(("grp", "sub")),
        P(None, ("grp", "sub")),
        P(("grp", "sub")),
        P(),
        P(("grp", "sub"), None, None, None),
        P(("grp", "sub"), None, None, None),
        P(("grp", "sub"), None, None),
        P(("grp", "sub"), None),
        P(("grp", "sub")),
    )
    return jax.shard_map(
        functools.partial(shards, mesh.shape["grp"], mesh.shape["sub"]),
        mesh=mesh,
        in_specs=placed,
        out_specs=(P(None, ("grp", "sub")), P(None, ("grp", "sub")), P()),
        check_vma=False,
    )
```

```python
import functools
import math

import jax
import jax.numpy as jnp
from jax import lax
from jax.experimental import pallas as pl
from jax.experimental.pallas import tpu as pltpu
from jax.sharding import PartitionSpec as P

MESH = pl.DeviceIdType.MESH
VMEM_BYTES = 60 * 1024 * 1024


def kernel(
    groups,
    subs,
    norm_scale,
    state_hbm,
    ocean_area_hbm,
    flux_hbm,
    atm_area_hbm,
    coupling_hbm,
    weight_hbm,
    block_hbm,
    count_hbm,
    link_slot_hbm,
    link_count_hbm,
    state_out,
    flux_out,
    imbalance_out,
    state_in,
    ocean_area_in,
    flux_in,
    atm_area_in,
    coupling_in,
    weight_in,
    block_in,
    count_in,
    link_slot_in,
    link_count_in,
    picked,
    read_slot,
    state_wide,
    state_send,
    state_recv,
    arrived,
    area_send,
    area_recv,
    parts,
    slot_hits,
    chooser,
    flux_send,
    flux_recv,
    totals,
    load_sem,
    state_sems,
    area_sems,
    flux_sems,
    total_sems,
):
    f32, bf16, i32 = jnp.float32, jnp.bfloat16, jnp.int32
    ocean_blocks = ocean_area_hbm.shape[0]
    fields_ocean = state_wide.shape[1]
    width = state_wide.shape[2]
    fields_atm = flux_in.shape[0]
    atm_blocks, link_total = weight_in.shape[:2]
    capacity = block_in.shape[3]
    routes = 3 * subs
    links = atm_blocks * link_total
    quad_rows = 4 * capacity
    flux_rows = flux_send.shape[1]
    me_grp = lax.axis_index("grp")
    me_sub = lax.axis_index("sub")

    pairs = [
        (block_hbm, block_in),
        (count_hbm, count_in),
        (state_hbm, state_in),
        (ocean_area_hbm, ocean_area_in.at[pl.ds(0, ocean_area_hbm.shape[0])]),
        (link_slot_hbm, link_slot_in),
        (link_count_hbm, link_count_in),
        (coupling_hbm, coupling_in),
        (flux_hbm, flux_in),
        (atm_area_hbm, atm_area_in),
        (weight_hbm, weight_in),
    ]
    loads = [
        pltpu.make_async_copy(source, target, load_sem.at[n])
        for n, (source, target) in enumerate(pairs)
    ]
    for load in loads[:3]:
        load.start()

    far = 2 * lax.rem(me_grp, 2)
    order = (far, 2 - far, 1)
    steps = [(o, t) for o in order[:2] for t in range(subs)] + [(1, t) for t in range(1, subs)]

    def grp_at(offset):
        return lax.rem(me_grp + offset + groups, groups)

    def sub_at(t):
        return lax.rem(me_sub + t, subs)

    barrier = pltpu.get_barrier_semaphore()
    others = groups * subs - 1

    def each_other(visit):
        def body(n, carry):
            visit((grp_at(n // subs), sub_at(n % subs)))
            return carry

        lax.fori_loop(1, others + 1, body, 0, unroll=others < 64)

    def greet(partner):
        pl.semaphore_signal(barrier, inc=1, device_id=partner, device_id_type=MESH)

    each_other(greet)

    for load in loads[3:]:
        load.start()

    def exchange(source, target, sems, o, t):
        k = sub_at(t)
        return pltpu.make_async_remote_copy(
            src_ref=source.at[o * subs + k],
            dst_ref=target.at[(2 - o) * subs + me_sub],
            send_sem=sems.at[0],
            recv_sem=sems.at[1],
            device_id=(grp_at(o - 1), k),
            device_id_type=MESH,
        )

    def drain(buffer, sem, count):
        ref = buffer.at[pl.ds(0, count)]
        pltpu.make_async_copy(ref, ref, sem).wait()

    loads[2].wait()
    for b in range(ocean_blocks):
        state_wide[b] = state_in[:, b * width : (b + 1) * width].astype(f32)
    state_wide[ocean_blocks] = jnp.zeros((fields_ocean, width), f32)

    loads[0].wait()
    loads[1].wait()

    def block_at(o, k, c):
        return jnp.where(c < count_in[o, 0, k], block_in[0, o, k, c], ocean_blocks)

    for o in range(3):
        for k in range(subs):
            for c in range(capacity):
                picked[(o * subs + k) * capacity + c] = block_at(o, k, c)

    for n, o in enumerate(order):
        for k in range(subs):
            first = (o * subs + k) * capacity
            rows = [state_wide[picked[first + c]] for c in range(capacity)]
            state_send[o * subs + k] = jnp.concatenate(rows, axis=0).astype(bf16)
        if n == 0:
            pl.semaphore_wait(barrier, others)
        for t in range(n // 2, subs):
            exchange(state_send, state_recv, state_sems, o, t).start()
    state_recv[subs + me_sub] = state_send[subs + me_sub]

    loads[3].wait()
    ocean_area_in[ocean_blocks] = jnp.zeros((1, width), f32)
    for n, o in enumerate(order):
        for k in range(subs):
            p = o * subs + k
            for c in range(capacity):
                area_send[p, c : c + 1, :] = ocean_area_in[picked[p * capacity + c]]
        for t in range(n // 2, subs):
            exchange(area_send, area_recv, area_sems, o, t).start()
    area_recv[subs + me_sub] = area_send[subs + me_sub]

    for n in range(4, 9):
        loads[n].wait()
    lane = lax.broadcasted_iota(i32, (1, 4 * links), 1)
    link_of = lane % links
    quad_of = lane // links
    key = jnp.full((1, 4 * links), -1, i32)
    for a in range(atm_blocks):
        for l in range(link_total):
            slot = link_slot_in[a, l]
            used = l < link_count_in[a]
            read_slot[a * link_total + l] = jnp.where(used, slot, routes * capacity)
            row = (slot // capacity) * quad_rows + slot % capacity
            row = jnp.where(used, row, -quad_rows)
            key = jnp.where(link_of == a * link_total + l, row, key)
    key = key + quad_of * capacity
    key = jnp.where(key < 0, -1, key)
    row_of = lax.broadcasted_iota(i32, (routes * quad_rows, 4 * links), 0)
    slot_hits[...] = jnp.where(row_of == key, 1.0, 0.0).astype(bf16)

    row_of = lax.broadcasted_iota(i32, (16, fields_atm), 0)
    lane_of = lax.broadcasted_iota(i32, (16, fields_atm), 1)
    arrived[routes * capacity] = jnp.zeros((fields_ocean, width), f32)
    coefficient = []
    for f in range(fields_ocean):
        spread = jnp.where(row_of == lane_of, coupling_in[f : f + 1, :], 0.0)
        column = jnp.sum(spread, axis=1, keepdims=True)
        coefficient.append(jnp.broadcast_to(column, (16, width)))

    drain(state_recv, state_sems.at[1], len(steps))
    loads[9].wait()
    for p in range(routes):
        arrived[p * capacity : (p + 1) * capacity] = (
            state_recv[p].astype(f32).reshape(capacity, fields_ocean, width)
        )

    pairs = [(a, a + 1) for a in range(0, atm_blocks, 2)]

    def weight_of(pair):
        return jnp.concatenate(
            [weight_in[a].reshape(link_total * width, width) for a in pair], axis=1
        )

    sums = []
    for pair in pairs:
        taken = [
            jnp.concatenate([arrived[read_slot[a * link_total + l]] for a in pair], axis=0)
            for l in range(link_total)
        ]
        taken = jnp.concatenate(taken, axis=1).astype(bf16)
        both = jnp.dot(taken, weight_of(pair), preferred_element_type=f32)
        for n in range(2):
            sums.append(both[n * fields_ocean : (n + 1) * fields_ocean, n * width : (n + 1) * width])

    atm_acc = jnp.zeros((16, width), f32)
    margin = jnp.zeros((16 - fields_atm, width), f32)
    coupled = []
    for a, state_sum in enumerate(sums):
        here = slice(a * width, (a + 1) * width)
        state_out[:, here] = state_sum.astype(bf16)
        change = coefficient[0] * state_sum[0:1]
        for f in range(1, fields_ocean):
            change = change + coefficient[f] * state_sum[f : f + 1]
        value = jnp.concatenate([flux_in[:, here].astype(f32), margin], axis=0)
        coupled.append((value + change).astype(bf16))
        atm_acc = atm_acc + atm_area_in[a : a + 1, :] * coupled[a].astype(f32)

    none = jnp.zeros((16, width), bf16)
    for pair in pairs:
        left = jnp.concatenate([coupled[pair[0]], none], axis=0)
        right = jnp.concatenate([none, coupled[pair[1]]], axis=0)
        part = lax.dot_general(
            jnp.concatenate([left, right], axis=1),
            weight_of(pair),
            (((1,), (1,)), ((), ())),
            preferred_element_type=f32,
        )
        for n, a in enumerate(pair):
            for l in range(link_total):
                parts[pl.ds(a * link_total + l, fields_atm, stride=links), :] = part[
                    n * 16 : n * 16 + fields_atm, l * width : (l + 1) * width
                ]

    quads = []
    for q in range(fields_atm // 4):
        operand = parts[q * 4 * links : (q + 1) * 4 * links, :].astype(bf16)
        quads.append(jnp.dot(slot_hits[...], operand, preferred_element_type=f32))
    blank = jnp.zeros((flux_rows - fields_atm * capacity, width), f32)
    for p in range(routes):
        rows = [quad[p * quad_rows : (p + 1) * quad_rows] for quad in quads]
        flux_send[p] = jnp.concatenate(rows + [blank], axis=0).astype(bf16)
    for o, t in steps:
        exchange(flux_send, flux_recv, flux_sems, o, t).start()
    flux_recv[subs + me_sub] = flux_send[subs + me_sub]

    drain(area_recv, area_sems.at[1], len(steps))
    ocean_acc = [jnp.zeros((quad_rows, width), f32) for _ in quads]
    for p in range(routes):
        area = area_recv[p][:capacity]
        area = jnp.concatenate([area] * 4, axis=0)
        for q, quad in enumerate(quads):
            rounded = quad[p * quad_rows : (p + 1) * quad_rows].astype(bf16).astype(f32)
            ocean_acc[q] = ocean_acc[q] + rounded * area

    def to_lanes(column, group):
        rows = column.shape[0]
        row_of = lax.broadcasted_iota(i32, (rows, 128), 0) // group
        lane_of = lax.broadcasted_iota(i32, (rows, 128), 1)
        return jnp.sum(jnp.where(row_of == lane_of, column, 0.0), axis=0, keepdims=True)

    ocean_rows = jnp.concatenate(ocean_acc, axis=0)
    mine = to_lanes(jnp.sum(atm_acc, axis=1, keepdims=True), 1) - to_lanes(
        jnp.sum(ocean_rows, axis=1, keepdims=True), capacity
    )
    me = me_grp * subs + me_sub
    totals[me] = mine

    def tell(partner):
        pltpu.make_async_remote_copy(
            src_ref=totals.at[me],
            dst_ref=totals.at[me],
            send_sem=total_sems.at[0],
            recv_sem=total_sems.at[1],
            device_id=partner,
            device_id_type=MESH,
        ).start()

    each_other(tell)
    lane = lax.broadcasted_iota(i32, (1, routes * flux_rows), 1)
    inner = lane % flux_rows
    slot_of = (lane // flux_rows) * capacity + inner % capacity
    key = jnp.full((1, routes * flux_rows), -1, i32)
    for o in range(3):
        for k in range(subs):
            for c in range(capacity):
                block = jnp.where(c < count_in[o, 0, k], block_in[0, o, k, c] * 16, -32)
                key = jnp.where(slot_of == (o * subs + k) * capacity + c, block, key)
    key = key + inner // capacity
    key = jnp.where(inner < fields_atm * capacity, key, -1)
    for part in range(4):
        rows = ocean_blocks * 4
        row_of = lax.broadcasted_iota(i32, (rows, routes * flux_rows), 0) + part * rows
        chooser[part * rows : (part + 1) * rows, :] = jnp.where(row_of == key, 1.0, 0.0).astype(
            bf16
        )
    drain(state_send, state_sems.at[0], len(steps))
    drain(area_send, area_sems.at[0], len(steps))

    drain(flux_recv, flux_sems.at[1], len(steps))
    returned = flux_recv[...].reshape(routes * flux_rows, width)
    flux_sum = jnp.dot(chooser[...], returned, preferred_element_type=f32)
    for b in range(ocean_blocks):
        flux_out[:, b * width : (b + 1) * width] = flux_sum[
            b * 16 : b * 16 + fields_atm
        ].astype(bf16)

    drain(totals, total_sems.at[1], others)
    imbalance_out[...] = jnp.sum(totals[...], axis=0) * norm_scale
    drain(flux_send, flux_sems.at[0], len(steps))
    drain(totals, total_sems.at[0], others)


def finish(state_in, flux_in, total_in, state_out, flux_out, total_out, sems):
    copies = [
        pltpu.make_async_copy(flux_in, flux_out, sems.at[0]),
        pltpu.make_async_copy(state_in, state_out, sems.at[1]),
    ]
    for copy in copies:
        copy.start()
    total_out[...] = total_in[0, : total_out.shape[0]]
    for copy in copies:
        copy.wait()


def shards(
    groups,
    subs,
    ocean_state,
    ocean_area,
    atm_flux,
    atm_area,
    coupling,
    remap_weight,
    send_block,
    send_count,
    link_slot,
    link_count,
):
    f32, bf16, i32 = jnp.float32, jnp.bfloat16, jnp.int32
    fields_ocean = ocean_state.shape[0]
    fields_atm = atm_flux.shape[0]
    atm_blocks, link_total, width = remap_weight.shape[:3]
    ocean_blocks = ocean_state.shape[1] // width
    capacity = send_block.shape[3]
    routes = 3 * subs
    links = atm_blocks * link_total
    flux_rows = -(-fields_atm * capacity // 16) * 16
    norm_scale = 1.0 / math.sqrt(groups * subs * atm_blocks * width)
    anywhere = pl.BlockSpec(memory_space=pl.ANY)
    vmem = pl.BlockSpec(memory_space=pltpu.VMEM)
    state_on_atm, flux_on_ocean, imbalance = pl.pallas_call(
        functools.partial(kernel, groups, subs, norm_scale),
        out_shape=(
            pltpu.VMEM((fields_ocean, atm_blocks * width), bf16),
            pltpu.VMEM((fields_atm, ocean_blocks * width), bf16),
            pltpu.VMEM((1, 128), f32),
        ),
        in_specs=[anywhere] * 10,
        out_specs=(vmem, vmem, vmem),
        scratch_shapes=[
            pltpu.VMEM(ocean_state.shape, bf16),
            pltpu.VMEM((ocean_blocks + 1, 1, width), f32),
            pltpu.VMEM(atm_flux.shape, bf16),
            pltpu.VMEM((atm_blocks, width), f32),
            pltpu.VMEM((fields_ocean, fields_atm), f32),
            pltpu.VMEM(remap_weight.shape, bf16),
            pltpu.SMEM(send_block.shape, i32),
            pltpu.SMEM((3, 1, subs), i32),
            pltpu.SMEM(link_slot.shape, i32),
            pltpu.SMEM(link_count.shape, i32),
            pltpu.SMEM((routes * capacity,), i32),
            pltpu.SMEM((links,), i32),
            pltpu.VMEM((ocean_blocks + 1, fields_ocean, width), f32),
            pltpu.VMEM((routes, capacity * fields_ocean, width), bf16),
            pltpu.VMEM((routes, capacity * fields_ocean, width), bf16),
            pltpu.VMEM((routes * capacity + 1, fields_ocean, width), f32),
            pltpu.VMEM((routes, 8, width), f32),
            pltpu.VMEM((routes, 8, width), f32),
            pltpu.VMEM((fields_atm * links, width), f32),
            pltpu.VMEM((routes * 4 * capacity, 4 * links), bf16),
            pltpu.VMEM((ocean_blocks * 16, routes * flux_rows), bf16),
            pltpu.VMEM((routes, flux_rows, width), bf16),
            pltpu.VMEM((routes, flux_rows, width), bf16),
            pltpu.VMEM((groups * subs, 1, 128), f32),
            pltpu.SemaphoreType.DMA((10,)),
            pltpu.SemaphoreType.DMA((2,)),
            pltpu.SemaphoreType.DMA((2,)),
            pltpu.SemaphoreType.DMA((2,)),
            pltpu.SemaphoreType.DMA((2,)),
        ],
        compiler_params=pltpu.CompilerParams(
            collective_id=0, has_side_effects=True, vmem_limit_bytes=VMEM_BYTES
        ),
    )(
        ocean_state,
        ocean_area.reshape(ocean_blocks, 1, width),
        atm_flux,
        atm_area.reshape(atm_blocks, width),
        coupling.T,
        remap_weight,
        send_block,
        send_count.reshape(3, 1, subs),
        link_slot,
        link_count,
    )
    return pl.pallas_call(
        finish,
        out_shape=(
            jax.ShapeDtypeStruct(state_on_atm.shape, bf16),
            jax.ShapeDtypeStruct(flux_on_ocean.shape, bf16),
            jax.ShapeDtypeStruct((fields_atm,), f32),
        ),
        in_specs=[vmem, vmem, vmem],
        out_specs=(anywhere, anywhere, vmem),
        scratch_shapes=[pltpu.SemaphoreType.DMA((2,))],
        compiler_params=pltpu.CompilerParams(vmem_limit_bytes=1024 * 1024),
    )(state_on_atm, flux_on_ocean, imbalance)


def solution(mesh):
    placed = (
        P(None, ("grp", "sub")),
        P(("grp", "sub")),
        P(None, ("grp", "sub")),
        P(("grp", "sub")),
        P(),
        P(("grp", "sub"), None, None, None),
        P(("grp", "sub"), None, None, None),
        P(("grp", "sub"), None, None),
        P(("grp", "sub"), None),
        P(("grp", "sub")),
    )
    return jax.shard_map(
        functools.partial(shards, mesh.shape["grp"], mesh.shape["sub"]),
        mesh=mesh,
        in_specs=placed,
        out_specs=(P(None, ("grp", "sub")), P(None, ("grp", "sub")), P()),
        check_vma=False,
    )
```
